256 devices in a mesh: group: 8 (over y_lo, x), leaf: 32 (over z, y_hi, core).
Axes of the slice: x: 4, y: 4 (y_hi: 2, y_lo: 2; y = y_hi * 2 + y_lo), z: 8, core: 2. Of those that a mesh axis runs over, the one named last changes fastest.
Arguments:
- points: bfloat16 [262144, 128], P(('group', 'leaf')), may hold values from -7 to 7
- vectors: bfloat16 [262144, 64], P(('group', 'leaf')), may hold values from -1.5 to 1.5
- leaf_interp: bfloat16 [262144, 128], P(('group', 'leaf')), may hold values from -0.5 to 0.5
- leaf_skeleton: int32 [32768], P(('group', 'leaf')), may hold values from 0 to 1023, as said below
- group_transfer: bfloat16 [32768, 512], P(('group', 'leaf')), may hold values from -0.25 to 0.25
- group_skeleton: int32 [4096], P('group'), may hold values from 0 to 4095, as said below
Outputs:
- product: float32 [262144, 64], P(('group', 'leaf'))
- basis: float32 [262144, 64], P(('group', 'leaf'))
The draws below stay inside these ranges and needn't reach their ends.
Inputs may be any that keep to these rules, and one draw needn't show every extreme that they name: `leaf_skeleton`: each leaf's 128 entries are different positions among that leaf's 1024 points, in ascending order. `group_skeleton`: each group's 512 entries are different positions, in ascending order, among the group's leaf skeleton points, numbered leaf by leaf with 128 to a leaf.
All inputs are finite; a program needn't handle non-finite values.
Results may differ from the reference program's by a relative error of at most 0.0081.
Values may be sent and summed in bfloat16 or wider, within the bound.
A program may use at most 64 MiB of HBM per device.

```python
import math
import jax
import jax.numpy as jnp
from jax import lax

D = 128
R = 64
LSK = 128
GSK = 512
LEAF_PTS = 1024
GROUPS = 8
LEAVES = 256
POINTS = 262144


def clipped_normal(key_val, shape):
    return jnp.clip(jax.random.normal(key_val, shape, jnp.float32), -4.0, 4.0)


def pick_sorted(key_val, count, pool, chosen):
    keys_all = jax.random.split(key_val, count)
    picked = jax.vmap(lambda one_key: jax.random.permutation(one_key, pool)[:chosen])(keys_all)
    ordered = jnp.sort(picked, axis=1)
    ordered = ordered.at[0, 0].set(0).at[0, chosen - 1].set(pool - 1)
    return ordered.reshape(-1).astype(jnp.int32)


def draw_points(key, part):
    key = jax.random.fold_in(key, 21)
    group_key, leaf_key, jitter_key = jax.random.split(key, 3)
    per_group = LEAVES // GROUPS
    group_center = clipped_normal(group_key, (GROUPS, 1, 1, D))
    leaf_center = clipped_normal(leaf_key, (GROUPS, per_group, 1, D))
    jitter = clipped_normal(jitter_key, (GROUPS, per_group, LEAF_PTS, D))
    mixed = 0.5 * group_center + 0.5 * leaf_center + 0.70710678 * jitter
    return mixed.reshape(POINTS, D).astype(jnp.bfloat16)


def draw_vectors(key, part):
    key = jax.random.fold_in(key, 22)
    base_key, scale_key = jax.random.split(key, 2)
    base_vals = clipped_normal(base_key, (POINTS, R))
    position = jnp.arange(POINTS, dtype=jnp.float32) / POINTS
    rising = jnp.exp(math.log(3.0) * position)[:, None]
    spread = jnp.exp(jax.random.uniform(scale_key, (POINTS, 1), jnp.float32, 0.0, math.log(4.0)))
    return (0.03 * rising * spread * base_vals).astype(jnp.bfloat16)


def draw_leaf_skeleton(key, part):
    key = jax.random.fold_in(key, 23)
    return pick_sorted(key, LEAVES, LEAF_PTS, LSK)


def draw_group_skeleton(key, part):
    key = jax.random.fold_in(key, 24)
    return pick_sorted(key, GROUPS, LEAVES // GROUPS * LSK, GSK)


def levels(stream_key, dims, pieces, smallest, high):
    def one(dim, shards_of):
        draws = jax.random.uniform(jax.random.fold_in(jax.random.fold_in(stream_key, 6), dim), (shards_of,), jnp.float32, smallest / len(pieces), high / len(pieces))
        return jnp.repeat(jnp.exp(draws), dims[dim] // shards_of).reshape((-1,) + (1,) * (len(dims) - dim - 1))

    gain = one(*pieces[0])
    for cut in pieces[1:]:
        gain = gain * one(*cut)
    return gain


def scatter_about(own_key, dims, width, limit, shards=(), kind=jnp.bfloat16):
    loudness = levels(own_key, dims, shards, -0.22, 0.18) if shards else 1.0
    array = jax.random.normal(own_key, dims, jnp.float32) * width * loudness
    return jnp.minimum(jnp.maximum(array, -limit), limit).astype(kind)


def setup_inputs(seed: int = 0) -> dict:
    splits = jax.random.split(jax.random.key(seed), 7)
    return {
        "points": draw_points(jax.random.fold_in(splits[6], 71), 0),
        "vectors": draw_vectors(jax.random.fold_in(splits[6], 71), 0),
        "leaf_interp": scatter_about(splits[2], (POINTS, LSK), LSK ** -0.5, 0.5, ((0, 256),)),
        "leaf_skeleton": draw_leaf_skeleton(jax.random.fold_in(splits[6], 71), 0),
        "group_transfer": scatter_about(splits[4], (LEAVES * LSK, GSK), GSK ** -0.5, 0.25, ((0, 256),)),
        "group_skeleton": draw_group_skeleton(jax.random.fold_in(splits[6], 71), 0),
    }


def kernel_block(queries, query_norms, key_rows, weights):
    key_norm_values = lax.optimization_barrier(jnp.sum(jnp.square(key_rows.astype(jnp.float32)), axis=1))
    inner_prod = jnp.dot(queries.astype(jnp.float32), key_rows.T.astype(jnp.float32), preferred_element_type=jnp.float32)
    squared_distance = query_norms[:, None] + key_norm_values[None, :] - 2.0 * inner_prod
    kernel_vals = jnp.exp(squared_distance * (-2.0 / D)).astype(jnp.bfloat16)
    return jnp.dot(kernel_vals.astype(jnp.float32), weights.astype(jnp.float32), preferred_element_type=jnp.float32)

def reference(points, vectors, leaf_interp, leaf_skeleton, group_transfer, group_skeleton):
    per_group = LEAVES // GROUPS
    leaf_points = points.reshape(LEAVES, LEAF_PTS, D)
    leaf_vector_rows = vectors.reshape(LEAVES, LEAF_PTS, R)
    leaf_interpolants = leaf_interp.reshape(LEAVES, LEAF_PTS, LSK)
    leaf_picks = leaf_skeleton.reshape(LEAVES, LSK).astype(jnp.int32)
    skel_points = jax.vmap(lambda leaf_rows, picks: jnp.take(leaf_rows, picks, axis=0))(leaf_points, leaf_picks)
    skeleton_weight = jnp.einsum('jba,jbz->jaz', leaf_interpolants.astype(jnp.float32), leaf_vector_rows.astype(jnp.float32)).astype(jnp.bfloat16)
    group_flat_points = skel_points.reshape(GROUPS, per_group * LSK, D)
    group_flat_weights = skeleton_weight.reshape(GROUPS, per_group * LSK, R)
    group_picks = group_skeleton.reshape(GROUPS, GSK).astype(jnp.int32)
    group_points = jax.vmap(lambda group_rows, picks: jnp.take(group_rows, picks, axis=0))(group_flat_points, group_picks)
    transfer = group_transfer.reshape(GROUPS, per_group * LSK, GSK)
    group_weights = jnp.einsum('grc,grv->gcv', transfer.astype(jnp.float32), group_flat_weights.astype(jnp.float32)).astype(jnp.bfloat16)
    all_group_points = group_points.reshape(GROUPS * GSK, D)
    all_group_weights = group_weights.reshape(GROUPS * GSK, R)
    row_group = jnp.arange(GROUPS * GSK, dtype=jnp.int32) // GSK
    skel_owner = jnp.arange(per_group * LSK, dtype=jnp.int32) // LSK

    def one_leaf(leaf_id):
        group_id = leaf_id // per_group
        local_leaf = leaf_id % per_group
        sibling = leaf_id ^ 1
        queries = leaf_points[leaf_id]
        query_norms = lax.optimization_barrier(jnp.sum(jnp.square(queries.astype(jnp.float32)), axis=1))
        result = kernel_block(queries, query_norms, queries, leaf_vector_rows[leaf_id])
        result = result + kernel_block(queries, query_norms, leaf_points[sibling], leaf_vector_rows[sibling])
        kept_rows = (skel_owner != local_leaf) & (skel_owner != local_leaf ^ 1)
        near_weights = group_flat_weights[group_id]
        near_weights = jnp.where(kept_rows[:, None], near_weights, jnp.zeros_like(near_weights))
        result = result + kernel_block(queries, query_norms, group_flat_points[group_id], near_weights)
        far_weights = jnp.where((row_group != group_id)[:, None], all_group_weights, jnp.zeros_like(all_group_weights))
        result = result + kernel_block(queries, query_norms, all_group_points, far_weights)
        return result
    product = lax.map(one_leaf, jnp.arange(LEAVES, dtype=jnp.int32)).reshape(POINTS, R)
    gram = lax.dot_general(product, product, (((0,), (0,)), ((), ())), precision=lax.Precision.HIGHEST)
    lower = jnp.linalg.cholesky(gram)
    solved = jax.scipy.linalg.solve_triangular(lower, product.T, lower=True).T
    basis = solved * math.sqrt(POINTS)
    return (product, basis)
```

```python
import math

import jax
import jax.numpy as jnp
from jax import lax
from jax.experimental import pallas as pl
from jax.experimental.pallas import tpu as pltpu
from jax.sharding import PartitionSpec as P

MESH = pl.DeviceIdType.MESH
F32 = jnp.float32
BF16 = jnp.bfloat16
NX, NYL, NZ, NYH = 4, 2, 8, 2
D = 128
R = 64
N = 1024
KR = 144
BR = KR + R
NEAR = [
    (1, 0), (7, 0), (0, 1), (2, 0), (6, 0), (1, 1), (7, 1), (3, 0),
    (5, 0), (4, 0), (2, 1), (6, 1), (3, 1), (5, 1), (4, 1),
]
FAR = [(dx, dyl, dyh) for dyl in range(2) for dx in (0, 1, 3, 2) if (dx, dyl) != (0, 0) for dyh in range(2)]
PLANE = [(dx, dyl, dyh) for dyl in range(2) for dyh in range(2) for dx in range(4) if (dx, dyl, dyh) != (0, 0, 0)]
NEAR0 = 16
FAR0 = 48
SLOTS = 80


def dot(a, b, ca=1, cb=0, precision=None):
    return lax.dot_general(
        a, b, (((ca,), (cb,)), ((), ())), preferred_element_type=F32, precision=precision
    )


def norm_rows(key_t, as_query):
    keys = key_t.astype(F32)
    norms = jnp.sum(keys * keys, axis=0, keepdims=True) * (-1.0 / 64.0)
    high = norms.astype(BF16).astype(F32)
    rest = norms - high
    mid = rest.astype(BF16).astype(F32)
    low = rest - mid
    row = lax.broadcasted_iota(jnp.int32, (16, key_t.shape[1]), 0)
    if as_query:
        row = jnp.where(row < 6, lax.rem(row + 3, 6), row)
    out = jnp.where(row == 0, high, jnp.where(row == 1, mid, jnp.where(row == 2, low, 0.0)))
    return jnp.where((row >= 3) & (row < 6), 1.0, out).astype(BF16)


def main_kernel(
    pts_hbm, vec_hbm, interp_hbm, lsk_hbm, trans_hbm, gsk_hbm,
    prod_ref, gram_ref,
    pts, vec, interp, lsk, trans, gsk, buf, own, far_own, q, acc,
    gw, gw_in, gp, gp_in, rsw, rsp, wq, pq, g_loc, g_sib, g_z, g_p, g_half,
    load_sem, sib_s, sib_r, near_s, near_r, nyh_s, nfw_s, nfw_r, rs_s, rs_r, zg_s, zg_r,
    far_s, far_r, ffw_s, ffw_r, gz_s, gz_r, gp_s, gp_r,
):
    grp = lax.axis_index("group")
    leaf = lax.axis_index("leaf")
    x, yl = lax.rem(grp, NX), grp // NX
    core, yh, z = lax.rem(leaf, 2), lax.rem(leaf // 2, 2), leaf // 4

    def dev(dx=0, dyl=0, dz=0, dyh=0, dc=0):
        return (
            lax.rem(yl + dyl, NYL) * NX + lax.rem(x + dx, NX),
            lax.rem(z + dz, NZ) * 4 + lax.rem(yh + dyh, 2) * 2 + lax.rem(core + dc, 2),
        )

    def remote(src, dst, ss, rs, to):
        return pltpu.make_async_remote_copy(
            src_ref=src, dst_ref=dst, send_sem=ss, recv_sem=rs, device_id=to, device_id_type=MESH
        )

    loads = [
        pltpu.make_async_copy(s, d, load_sem.at[i])
        for i, (s, d) in enumerate(
            ((pts_hbm, pts), (lsk_hbm, lsk), (vec_hbm, vec), (interp_hbm, interp), (trans_hbm, trans), (gsk_hbm, gsk))
        )
    ]
    for c in loads:
        c.start()
    barrier = pltpu.get_barrier_semaphore()
    peers = [dev(dc=1)]
    peers += [dev(dz=dz, dyh=dyh) for dz, dyh in NEAR]
    peers += [dev(dx=dx, dyl=dyl, dyh=dyh) for dx, dyl, dyh in FAR]
    for p in peers:
        pl.semaphore_signal(barrier, inc=1, device_id=p, device_id_type=MESH)
    sib = dev(dc=1)
    sent = []

    for c in loads:
        c.wait()
    pts_t = jnp.transpose(pts[...])
    hot = (lax.broadcasted_iota(jnp.int32, (N, D), 0) == lsk[...]).astype(F32).astype(BF16)
    skel_t = dot(pts_t, hot).astype(BF16)
    own[0:D, :] = skel_t
    own[D:KR, :] = norm_rows(skel_t, False)
    w_t = dot(vec[...], interp[...])
    own[KR:BR, :] = w_t.astype(BF16)
    w = jnp.transpose(w_t).astype(BF16)
    trans_t = jnp.transpose(trans[...])
    for k in range(4):
        gw[pl.ds(k * 64, 64), 0:R] = dot(trans_t[k * 128 : k * 128 + 64], w)
        gw[pl.ds(k * 64, 64), R : 2 * R] = dot(trans_t[k * 128 + 64 : k * 128 + 128], w)
        pick = lax.broadcasted_iota(jnp.int32, (D, D), 0) + leaf * D == gsk[:, k * D : (k + 1) * D]
        gp[k] = dot(skel_t, pick.astype(F32).astype(BF16)).astype(BF16)
    key_norms = norm_rows(pts_t, False)
    for k in range(8):
        s = slice(k * D, (k + 1) * D)
        buf[k, 0:D, :] = pts_t[:, s]
        buf[k, D:KR, :] = key_norms[:, s]
        buf[k, KR:BR, :] = vec[:, s]
    q[:, 0:D] = pts[...] * jnp.asarray(1.0 / 32.0, BF16)
    q[:, D:KR] = jnp.transpose(norm_rows(pts_t, True))
    acc[...] = jnp.zeros_like(acc)
    for s in (46, 47, 76, 77, 78, 79):
        buf[s] = jnp.zeros((BR, D), BF16)

    pl.semaphore_wait(barrier, len(peers))

    other = 1 - core
    sib_w = remote(gw.at[pl.ds(other * 128, 128)], gw_in, sib_s.at[0], sib_r.at[0], sib)
    sib_p = remote(gp.at[pl.ds(other * 2, 2)], gp_in, sib_s.at[1], sib_r.at[1], sib)
    sib_x = remote(buf.at[pl.ds(0, 8)], buf.at[pl.ds(8, 8)], sib_s.at[2], sib_r.at[2], sib)
    for c in (sib_w, sib_p, sib_x):
        c.start()

    def near_slot(k):
        return buf.at[NEAR0 + 2 * k]

    def near_copy(k):
        dz, dyh = NEAR[k]
        return remote(own, near_slot(k), near_s.at[k], near_r.at[k], dev(dz=dz and NZ - dz, dyh=dyh))

    def near_yh(k):
        dz, _ = NEAR[k]
        j = NEAR.index((dz, 1))
        return remote(near_slot(k), near_slot(j), nyh_s.at[k], near_r.at[j], dev(dyh=1))

    def near_fwd(k):
        return remote(near_slot(k), buf.at[NEAR0 + 2 * k + 1], nfw_s.at[k], nfw_r.at[k], sib)

    def start(make, *args):
        make(*args).start()
        sent.append((make, args))

    def near_arrived(k):
        near_copy(k).wait_recv()
        start(near_fwd, k)
        if NEAR[k][1] == 0:
            start(near_yh, k)

    def rs_to(k):
        dz, dyh = NEAR[k]
        return dev(dz=dz, dyh=dyh), lax.rem(z + dz, NZ), lax.rem(yh + dyh, 2)

    def rs_w(k):
        to, tz, ty = rs_to(k)
        src = gw.at[pl.ds(core * 128 + ty * 64 + tz * 8, 8)]
        return remote(src, rsw.at[k], rs_s.at[0, k], rs_r.at[0, k], to)

    def rs_p(k):
        to, tz, ty = rs_to(k)
        src = gp.at[core * 2 + ty, pl.ds(tz * 16, 16)]
        return remote(src, rsp.at[k], rs_s.at[1, k], rs_r.at[1, k], to)

    def zg_w(d):
        mine = wq.at[pl.ds(z * 8, 8)]
        return remote(mine, mine, zg_s.at[0, d], zg_r.at[0, d], dev(dz=d))

    def zg_p(d):
        mine = pq.at[pl.ds(z * 16, 16)]
        return remote(mine, mine, zg_s.at[1, d], zg_r.at[1, d], dev(dz=d))

    def zg_wait(d):
        fz = lax.rem(z + NZ - d, NZ)
        to = dev(dz=d)
        remote(wq.at[pl.ds(fz * 8, 8)], wq.at[pl.ds(fz * 8, 8)], zg_s.at[0, d], zg_r.at[0, d], to).wait_recv()
        remote(pq.at[pl.ds(fz * 16, 16)], pq.at[pl.ds(fz * 16, 16)], zg_s.at[1, d], zg_r.at[1, d], to).wait_recv()

    def far_copy(k):
        dx, dyl, dyh = FAR[k]
        return remote(
            far_own, buf.at[FAR0 + 2 * k], far_s.at[k], far_r.at[k],
            dev(dx=dx and NX - dx, dyl=dyl, dyh=dyh),
        )

    def far_fwd(k):
        return remote(buf.at[FAR0 + 2 * k], buf.at[FAR0 + 2 * k + 1], ffw_s.at[k], ffw_r.at[k], sib)

    def phase_sib():
        sib_w.wait_recv()
        sib_p.wait_recv()
        mine = pl.ds(core * 128, 128)
        gw[mine] = gw[mine] + gw_in[...]
        mine = pl.ds(core * 2, 2)
        gp[mine] = gp[mine] + gp_in[...]
        for k in range(15):
            start(rs_w, k)
            start(rs_p, k)
        for k in range(15):
            if NEAR[k][1] == 0 or NEAR[k][0] == 0:
                start(near_copy, k)
        sib_x.wait_recv()

    def phase_near0():
        for k in (0, 1, 2, 3, 4):
            near_arrived(k)
        for k in (0, 1, 2, 3):
            near_fwd(k).wait_recv()

    def phase_rs():
        for k in range(15):
            rs_w(k).wait_recv()
            rs_p(k).wait_recv()
        total = gw[pl.ds(core * 128 + yh * 64 + z * 8, 8)]
        rows = gp[core * 2 + yh, pl.ds(z * 16, 16)].astype(F32)
        for k in range(15):
            total = total + rsw[k]
            rows = rows + rsp[k].astype(F32)
        wq[pl.ds(z * 8, 8)] = total
        pq[pl.ds(z * 16, 16)] = rows.astype(BF16)
        for d in range(1, 8):
            start(zg_w, d)
            start(zg_p, d)
        for k in (7, 8, 5, 6):
            near_arrived(k)
        for k in (4, 5, 6, 7):
            near_fwd(k).wait_recv()

    def phase_near2():
        for k in (9, 10, 11):
            near_arrived(k)
        for k in (8, 9, 10, 11):
            near_fwd(k).wait_recv()

    def phase_zg():
        for d in range(1, 8):
            zg_wait(d)
        pq_v = pq[...]
        far_own[0:D, :] = pq_v
        far_own[D:KR, :] = norm_rows(pq_v, False)
        wq_t = jnp.transpose(wq[...])
        far_own[KR:BR, :] = jnp.concatenate([wq_t[0:R], wq_t[R : 2 * R]], axis=1).astype(BF16)
        for k in range(14):
            start(far_copy, k)
        for k in (12, 13, 14):
            near_arrived(k)
        for k in (12, 13, 14):
            near_fwd(k).wait_recv()

    def phase_far(lo, hi):
        def run():
            for k in range(lo, hi):
                far_copy(k).wait_recv()
                start(far_fwd, k)
            for k in range(lo, hi):
                far_fwd(k).wait_recv()

        return run

    phases = {
        1: phase_sib,
        2: phase_near0,
        3: phase_rs,
        4: phase_near2,
        5: phase_zg,
        6: phase_far(0, 4),
        7: phase_far(4, 8),
        8: phase_far(8, 12),
        9: phase_far(12, 14),
    }

    def chunk(i, carry):
        for n, phase in phases.items():
            pl.when(i == n)(phase)
        base = i * 8
        keys = jnp.concatenate([buf[base + j, 0:KR, :] for j in range(8)], axis=1)
        weights = jnp.concatenate([buf[base + j, KR:BR, :] for j in range(8)], axis=1)
        for t in range(4):
            rows = pl.ds(t * 256, 256)
            kernel_vals = jnp.exp(dot(q[rows, :], keys)).astype(BF16)
            acc[rows, :] += dot(kernel_vals, weights, 1, 1)
        return carry

    lax.fori_loop(0, 10, chunk, 0)

    prod_t = jnp.transpose(acc[...])
    prod_ref[...] = prod_t
    gram = dot(prod_t, acc[...], precision=lax.Precision.HIGHEST)
    g_loc[...] = jnp.concatenate([gram[0:32], gram[32:64]], axis=1)
    def gram_sib():
        return remote(g_loc.at[pl.ds(other * 16, 16)], g_sib, sib_s.at[3], sib_r.at[3], sib)

    def gram_z(d):
        return remote(g_z.at[z], g_z.at[z], gz_s.at[d], gz_r.at[d], dev(dz=d))

    def gram_plane(k):
        dx, dyl, dyh = PLANE[k]
        return remote(g_p.at[here], g_p.at[here], gp_s.at[k], gp_r.at[k], dev(dx=dx, dyl=dyl, dyh=dyh))

    def gram_back():
        mine = g_half.at[pl.ds(core * 16, 16)]
        return remote(mine, mine, sib_s.at[4], sib_r.at[4], sib)

    start(gram_sib)
    gram_sib().wait_recv()
    g_z[z] = g_loc[pl.ds(core * 16, 16)] + g_sib[...]
    for d in range(1, 8):
        start(gram_z, d)
    for d in range(1, 8):
        fz = lax.rem(z + NZ - d, NZ)
        remote(g_z.at[fz], g_z.at[fz], gz_s.at[d], gz_r.at[d], dev(dz=d)).wait_recv()
    total = g_z[0]
    for k in range(1, 8):
        total = total + g_z[k]
    here = (yl * 2 + yh) * 4 + x
    g_p[here] = total
    for k in range(15):
        start(gram_plane, k)
    for k, (dx, dyl, dyh) in enumerate(PLANE):
        there = (lax.rem(yl + dyl, 2) * 2 + lax.rem(yh + dyh, 2)) * 4 + lax.rem(x + NX - dx, NX)
        remote(
            g_p.at[there], g_p.at[there], gp_s.at[k], gp_r.at[k], dev(dx=dx, dyl=dyl, dyh=dyh)
        ).wait_recv()
    total = g_p[0]
    for k in range(1, 16):
        total = total + g_p[k]
    g_half[pl.ds(core * 16, 16)] = total
    start(gram_back)
    theirs = g_half.at[pl.ds(other * 16, 16)]
    remote(theirs, theirs, sib_s.at[4], sib_r.at[4], sib).wait_recv()
    gram_ref[...] = g_half[...]
    for c in (sib_w, sib_p, sib_x):
        c.wait_send()
    for make, args in sent:
        make(*args).wait_send()


def tail_kernel(prod_ref, gram_ref, out_ref, basis_ref, work):
    packed = gram_ref[...]
    gram = jnp.concatenate([packed[:, 0:R], packed[:, R : 2 * R]], axis=0)
    row = lax.broadcasted_iota(jnp.int32, (R, 2 * R), 0)
    lane = lax.broadcasted_iota(jnp.int32, (R, 2 * R), 1)
    work[...] = jnp.concatenate([gram, (row == lane).astype(F32)[:, 0:R]], axis=1)
    out_ref[...] = prod_ref[...]

    def step(k, scale):
        a = work[...]
        pivot = work[pl.ds(k, 1), :]
        col = jnp.sum(jnp.where(lane == k, a, 0.0), axis=1, keepdims=True)
        diag = jnp.sum(jnp.where(lane[0:1] == k, pivot, 0.0), axis=1, keepdims=True)
        factor = jnp.where(row[:, 0:1] > k, col / diag, 0.0)
        work[...] = a - factor * pivot
        return jnp.where(row[:, 0:1] == k, lax.rsqrt(diag), scale)

    scale = lax.fori_loop(0, R, step, jnp.zeros((R, 1), F32))
    inverse = work[:, R : 2 * R] * (scale * 512.0)
    basis_ref[...] = dot(inverse, prod_ref[...], precision=lax.Precision.HIGHEST)


def per_device(points, vectors, leaf_interp, leaf_skeleton, group_transfer, group_skeleton):
    hbm = pl.BlockSpec(memory_space=pl.ANY)
    vmem = pl.BlockSpec(memory_space=pltpu.VMEM)
    dma = pltpu.SemaphoreType.DMA
    prod_t, gram = pl.pallas_call(
        main_kernel,
        out_shape=(jax.ShapeDtypeStruct((R, N), F32), jax.ShapeDtypeStruct((32, 128), F32)),
        in_specs=[hbm] * 6,
        out_specs=(vmem, vmem),
        scratch_shapes=[
            pltpu.VMEM((N, D), BF16),
            pltpu.VMEM((R, N), BF16),
            pltpu.VMEM((N, D), BF16),
            pltpu.VMEM((1, 128), jnp.int32),
            pltpu.VMEM((128, 512), BF16),
            pltpu.VMEM((1, 512), jnp.int32),
            pltpu.VMEM((SLOTS, BR, D), BF16),
            pltpu.VMEM((BR, D), BF16),
            pltpu.VMEM((BR, D), BF16),
            pltpu.VMEM((N, KR), BF16),
            pltpu.VMEM((N, R), F32),
            pltpu.VMEM((256, 128), F32),
            pltpu.VMEM((128, 128), F32),
            pltpu.VMEM((4, 128, 128), BF16),
            pltpu.VMEM((2, 128, 128), BF16),
            pltpu.VMEM((15, 8, 128), F32),
            pltpu.VMEM((15, 16, 128), BF16),
            pltpu.VMEM((64, 128), F32),
            pltpu.VMEM((128, 128), BF16),
            pltpu.VMEM((32, 128), F32),
            pltpu.VMEM((16, 128), F32),
            pltpu.VMEM((8, 16, 128), F32),
            pltpu.VMEM((16, 16, 128), F32),
            pltpu.VMEM((32, 128), F32),
            dma((6,)),
            dma((5,)),
            dma((5,)),
            dma((15,)),
            dma((15,)),
            dma((15,)),
            dma((15,)),
            dma((15,)),
            dma((2, 15)),
            dma((2, 15)),
            dma((2, 8)),
            dma((2, 8)),
            dma((14,)),
            dma((14,)),
            dma((14,)),
            dma((14,)),
            dma((8,)),
            dma((8,)),
            dma((15,)),
            dma((15,)),
        ],
        compiler_params=pltpu.CompilerParams(
            collective_id=0, has_side_effects=True, vmem_limit_bytes=40 * 2**20
        ),
        name="hss_main",
    )(
        points,
        vectors.T,
        leaf_interp,
        leaf_skeleton.reshape(1, 128),
        group_transfer,
        group_skeleton.reshape(1, 512),
    )
    out_t, basis_t = pl.pallas_call(
        tail_kernel,
        out_shape=(jax.ShapeDtypeStruct((R, N), F32), jax.ShapeDtypeStruct((R, N), F32)),
        in_specs=[vmem, vmem],
        out_specs=(vmem, vmem),
        scratch_shapes=[pltpu.VMEM((R, 2 * R), F32)],
        compiler_params=pltpu.CompilerParams(vmem_limit_bytes=16 * 2**20),
        name="hss_tail",
    )(prod_t, gram)
    return out_t.T, basis_t.T


def solution(mesh):
    spec = P(("group", "leaf"), None)
    return jax.shard_map(
        per_device,
        mesh=mesh,
        in_specs=(spec, spec, spec, P(("group", "leaf")), spec, P("group")),
        out_specs=(spec, spec),
        check_vma=False,
    )
```

```python
import math

import jax
import jax.numpy as jnp
from jax import lax
from jax.experimental import pallas as pl
from jax.experimental.pallas import tpu as pltpu
from jax.sharding import PartitionSpec as P

MESH = pl.DeviceIdType.MESH
F32 = jnp.float32
BF16 = jnp.bfloat16
NX, NYL, NZ, NYH = 4, 2, 8, 2
D = 128
R = 64
N = 1024
KR = 144
BR = KR + R
NEAR = [
    (1, 0), (7, 0), (0, 1), (2, 0), (6, 0), (1, 1), (7, 1), (3, 0),
    (5, 0), (4, 0), (2, 1), (6, 1), (3, 1), (5, 1), (4, 1),
]
FAR = [
    ("y", 0, 1), ("y", 0, 3), ("x", 1, 0), ("x", 1, 1), ("x", 3, 0), ("x", 3, 1), ("y", 1, 1),
    ("y", 1, 3), ("y", 3, 1), ("y", 3, 3), ("x", 2, 0), ("x", 2, 1), ("y", 2, 1), ("y", 2, 3),
]
PLANE = [(dx, dyl, dyh) for dyl in range(2) for dyh in range(2) for dx in range(4) if (dx, dyl, dyh) != (0, 0, 0)]
NEAR0 = 16
FAR0 = 48
SLOTS = 80


def dot(a, b, ca=1, cb=0, precision=None):
    return lax.dot_general(
        a, b, (((ca,), (cb,)), ((), ())), preferred_element_type=F32, precision=precision
    )


def norm_rows(key_t, as_query):
    keys = key_t.astype(F32)
    norms = jnp.sum(keys * keys, axis=0, keepdims=True) * (-1.0 / 64.0)
    high = norms.astype(BF16).astype(F32)
    rest = norms - high
    mid = rest.astype(BF16).astype(F32)
    low = rest - mid
    row = lax.broadcasted_iota(jnp.int32, (16, key_t.shape[1]), 0)
    if as_query:
        row = jnp.where(row < 6, lax.rem(row + 3, 6), row)
    out = jnp.where(row == 0, high, jnp.where(row == 1, mid, jnp.where(row == 2, low, 0.0)))
    return jnp.where((row >= 3) & (row < 6), 1.0, out).astype(BF16)


def main_kernel(
    pts_hbm, vec_hbm, interp_hbm, lsk_hbm, trans_hbm, gsk_hbm,
    prod_ref, gram_ref,
    pts, vec, interp, lsk, trans, gsk, buf, own, far_own, q, acc,
    gw, gw_in, gp, gp_in, rsw, rsp, pair_in_w, pair_in_p, ag, g_loc, g_sib, g_z, g_p, g_half,
    load_sem, sib_s, sib_r, near_s, near_r, nyh_s, nfw_s, nfw_r, rs_s, rs_r, zg_s, zg_r,
    far_s, far_r, ffw_s, ffw_r, gz_s, gz_r, gp_s, gp_r,
):
    grp = lax.axis_index("group")
    leaf = lax.axis_index("leaf")
    x, yl = lax.rem(grp, NX), grp // NX
    core, yh, z = lax.rem(leaf, 2), lax.rem(leaf // 2, 2), leaf // 4

    def dev(dx=0, dyl=0, dz=0, dyh=0, dc=0):
        return (
            lax.rem(yl + dyl, NYL) * NX + lax.rem(x + dx, NX),
            lax.rem(z + dz, NZ) * 4 + lax.rem(yh + dyh, 2) * 2 + lax.rem(core + dc, 2),
        )

    def ydev(dy):
        y = lax.rem(yh * 2 + yl + dy, 4)
        return (lax.rem(y, 2) * NX + x, z * 4 + (y // 2) * 2 + core)

    def remote(src, dst, ss, rs, to):
        return pltpu.make_async_remote_copy(
            src_ref=src, dst_ref=dst, send_sem=ss, recv_sem=rs, device_id=to, device_id_type=MESH
        )

    loads = [
        pltpu.make_async_copy(s, d, load_sem.at[i])
        for i, (s, d) in enumerate(
            ((pts_hbm, pts), (lsk_hbm, lsk), (vec_hbm, vec), (interp_hbm, interp), (trans_hbm, trans), (gsk_hbm, gsk))
        )
    ]
    for c in loads:
        c.start()
    barrier = pltpu.get_barrier_semaphore()
    peers = [dev(dc=1)]
    peers += [dev(dz=d) for d in range(1, 8)] + [dev(dyh=1)]
    peers += [dev(dx=dx) for dx in (1, 2, 3)] + [ydev(1), ydev(3)]
    for p in peers:
        pl.semaphore_signal(barrier, inc=1, device_id=p, device_id_type=MESH)
    sib = dev(dc=1)
    sent = []

    for c in loads:
        c.wait()
    pts_t = jnp.transpose(pts[...])
    hot = (lax.broadcasted_iota(jnp.int32, (N, D), 0) == lsk[...]).astype(F32).astype(BF16)
    skel_t = dot(pts_t, hot).astype(BF16)
    own[0:D, :] = skel_t
    own[D:KR, :] = norm_rows(skel_t, False)
    w_t = dot(vec[...], interp[...])
    own[KR:BR, :] = w_t.astype(BF16)
    w = jnp.transpose(w_t).astype(BF16)
    trans_t = jnp.transpose(trans[...])
    for k in range(4):
        half, n = k // 2, k % 2
        left = dot(trans_t[k * 128 : k * 128 + 64], w)
        right = dot(trans_t[k * 128 + 64 : k * 128 + 128], w)
        pick = lax.broadcasted_iota(jnp.int32, (D, D), 0) + leaf * D == gsk[:, k * D : (k + 1) * D]
        picked = dot(skel_t, pick.astype(F32).astype(BF16)).astype(BF16)
        for t in range(NZ):
            gw[half, t, n * 8 : n * 8 + 8, 0:R] = left[t * 8 : t * 8 + 8]
            gw[half, t, n * 8 : n * 8 + 8, R : 2 * R] = right[t * 8 : t * 8 + 8]
            gp[half, t, n * 16 : n * 16 + 16, :] = picked[t * 16 : t * 16 + 16]
    key_norms = norm_rows(pts_t, False)
    for k in range(8):
        s = slice(k * D, (k + 1) * D)
        buf[k, 0:D, :] = pts_t[:, s]
        buf[k, D:KR, :] = key_norms[:, s]
        buf[k, KR:BR, :] = vec[:, s]
    q[:, 0:D] = pts[...] * jnp.asarray(1.0 / 32.0, BF16)
    q[:, D:KR] = jnp.transpose(norm_rows(pts_t, True))
    acc[...] = jnp.zeros_like(acc)
    for s in (46, 47, 76, 77, 78, 79):
        buf[s] = jnp.zeros((BR, D), BF16)

    pl.semaphore_wait(barrier, len(peers))

    other = 1 - core
    sib_w = remote(gw.at[other], gw_in, sib_s.at[0], sib_r.at[0], sib)
    sib_p = remote(gp.at[other], gp_in, sib_s.at[1], sib_r.at[1], sib)
    sib_x = remote(buf.at[pl.ds(0, 8)], buf.at[pl.ds(8, 8)], sib_s.at[2], sib_r.at[2], sib)
    for c in (sib_w, sib_p, sib_x):
        c.start()

    def near_slot(k):
        return buf.at[NEAR0 + 2 * k]

    def near_copy(k):
        dz, dyh = NEAR[k]
        return remote(own, near_slot(k), near_s.at[k], near_r.at[k], dev(dz=dz and NZ - dz, dyh=dyh))

    def near_yh(k):
        dz, _ = NEAR[k]
        j = NEAR.index((dz, 1))
        return remote(near_slot(k), near_slot(j), nyh_s.at[k], near_r.at[j], dev(dyh=1))

    def near_fwd(k):
        return remote(near_slot(k), buf.at[NEAR0 + 2 * k + 1], nfw_s.at[k], nfw_r.at[k], sib)

    def start(make, *args):
        make(*args).start()
        sent.append((make, args))

    def near_arrived(k):
        near_copy(k).wait_recv()
        start(near_fwd, k)
        if NEAR[k][1] == 0:
            start(near_yh, k)

    def rs_w(d):
        return remote(gw.at[core, lax.rem(z + d, NZ)], rsw.at[d], rs_s.at[0, d], rs_r.at[0, d], dev(dz=d))

    def rs_p(d):
        return remote(gp.at[core, lax.rem(z + d, NZ)], rsp.at[d], rs_s.at[1, d], rs_r.at[1, d], dev(dz=d))

    def pair_w():
        return remote(rsw.at[0], pair_in_w, sib_s.at[5], sib_r.at[5], dev(dyh=1))

    def pair_p():
        return remote(rsp.at[0], pair_in_p, sib_s.at[6], sib_r.at[6], dev(dyh=1))

    def zg(d):
        return remote(ag.at[z], ag.at[z], zg_s.at[d], zg_r.at[d], dev(dz=d))

    def zg_wait(d):
        theirs = ag.at[lax.rem(z + NZ - d, NZ)]
        remote(theirs, theirs, zg_s.at[d], zg_r.at[d], dev(dz=d)).wait_recv()

    def far_slot(k):
        return buf.at[FAR0 + 2 * k]

    def far_copy(k):
        axis, dx, n = FAR[k]
        if axis == "x":
            return remote(far_own.at[n], far_slot(k), far_s.at[k], far_r.at[k], dev(dx=NX - dx))
        quarter = 0 if n == 3 else 1
        src = far_own.at[quarter] if dx == 0 else far_slot(FAR.index(("x", dx, quarter)))
        return remote(src, far_slot(k), far_s.at[k], far_r.at[k], ydev(4 - n))

    def far_fwd(k):
        return remote(buf.at[FAR0 + 2 * k], buf.at[FAR0 + 2 * k + 1], ffw_s.at[k], ffw_r.at[k], sib)

    def phase_start():
        sib_w.wait_recv()
        sib_p.wait_recv()
        gw[core] = gw[core] + gw_in[...]
        gp[core] = gp[core] + gp_in[...]
        for d in range(1, 8):
            start(rs_w, d)
            start(rs_p, d)
        for k in (0, 1, 2, 3, 4):
            start(near_copy, k)

    def phase_sib():
        sib_x.wait_recv()

    def phase_rs():
        for d in range(1, 8):
            rs_w(d).wait_recv()
            rs_p(d).wait_recv()
        total = gw[core, z]
        rows = gp[core, z].astype(F32)
        for d in range(1, 8):
            total = total + rsw[d]
            rows = rows + rsp[d].astype(F32)
        rsw[0] = total
        rsp[0] = rows.astype(BF16)
        start(pair_w)
        start(pair_p)
        for k in (7, 8, 9):
            start(near_copy, k)

    def phase_pair():
        pair_w().wait_recv()
        pair_p().wait_recv()
        ag[z, 0:16, :] = (rsw[0] + pair_in_w[...]).astype(BF16)
        ag[z, 16:48, :] = rsp[0] + pair_in_p[...]
        for d in range(1, 8):
            start(zg, d)

    def near_phase(arrive, use):
        for k in arrive:
            near_arrived(k)
        for k in use:
            near_fwd(k).wait_recv()

    def phase_near0():
        near_phase((0, 1, 2, 3, 4), (0, 1, 2, 3))

    def phase_near1():
        near_phase((7, 8, 9, 5, 6), (4, 5, 6, 7))

    def phase_near2():
        near_phase((10, 11), (8, 9, 10, 11))

    def phase_near3():
        near_phase((12, 13, 14), (12, 13, 14))

    def phase_zg():
        for d in range(1, 8):
            zg_wait(d)
        for n in range(2):
            points_t = jnp.concatenate([ag[t, 16 + n * 16 : 32 + n * 16, :] for t in range(NZ)], axis=0)
            far_own[n, 0:D, :] = points_t
            far_own[n, D:KR, :] = norm_rows(points_t, False)
            pairs = jnp.concatenate(
                [ag[t, 0:16, :].astype(F32)[n * 8 : n * 8 + 8] for t in range(NZ)], axis=0
            )
            w_pairs = jnp.transpose(pairs)
            far_own[n, KR:BR, :] = jnp.concatenate([w_pairs[0:R], w_pairs[R : 2 * R]], axis=1).astype(BF16)
        for k, (axis, dx, _) in enumerate(FAR):
            if axis == "x" or dx == 0:
                start(far_copy, k)

    def phase_far(arrive, use):
        def far():
            for k in arrive:
                far_copy(k).wait_recv()
                start(far_fwd, k)
                axis, dx, n = FAR[k]
                if axis == "x":
                    start(far_copy, FAR.index(("y", dx, 3 if n == 0 else 1)))
            for k in use:
                far_fwd(k).wait_recv()

        return far

    with jax.named_scope("phase_start"):
        phase_start()
    phases = [
        (1, phase_sib),
        (2, phase_rs),
        (2, phase_near0),
        (3, phase_pair),
        (3, phase_near1),
        (4, phase_zg),
        (4, phase_near2),
        (5, phase_near3),
        (6, phase_far((0, 1, 2, 3, 4, 5), (0, 1, 2, 3))),
        (7, phase_far((10, 11, 6, 7), (4, 5, 6, 7))),
        (8, phase_far((8, 9), (8, 9, 10, 11))),
        (9, phase_far((12, 13), (12, 13))),
    ]

    def chunk(i, carry):
        for n, phase in phases:
            with jax.named_scope(phase.__name__):
                pl.when(i == n)(phase)
        base = i * 8
        keys = jnp.concatenate([buf[base + j, 0:KR, :] for j in range(8)], axis=1)
        weights = jnp.concatenate([buf[base + j, KR:BR, :] for j in range(8)], axis=1)
        for t in range(4):
            rows = pl.ds(t * 256, 256)
            kernel_vals = jnp.exp(dot(q[rows, :], keys)).astype(BF16)
            acc[rows, :] += dot(kernel_vals, weights, 1, 1)
        return carry

    lax.fori_loop(0, 10, chunk, 0)

    prod_t = jnp.transpose(acc[...])
    prod_ref[...] = prod_t
    gram = dot(prod_t, acc[...], precision=lax.Precision.HIGHEST)
    g_loc[...] = jnp.concatenate([gram[0:32], gram[32:64]], axis=1)
    def gram_sib():
        return remote(g_loc.at[pl.ds(other * 16, 16)], g_sib, sib_s.at[3], sib_r.at[3], sib)

    def gram_z(d):
        return remote(g_z.at[z], g_z.at[z], gz_s.at[d], gz_r.at[d], dev(dz=d))

    def gram_plane(k):
        dx, dyl, dyh = PLANE[k]
        return remote(g_p.at[here], g_p.at[here], gp_s.at[k], gp_r.at[k], dev(dx=dx, dyl=dyl, dyh=dyh))

    def gram_back():
        mine = g_half.at[pl.ds(core * 16, 16)]
        return remote(mine, mine, sib_s.at[4], sib_r.at[4], sib)

    start(gram_sib)
    gram_sib().wait_recv()
    g_z[z] = g_loc[pl.ds(core * 16, 16)] + g_sib[...]
    for d in range(1, 8):
        start(gram_z, d)
    for d in range(1, 8):
        fz = lax.rem(z + NZ - d, NZ)
        remote(g_z.at[fz], g_z.at[fz], gz_s.at[d], gz_r.at[d], dev(dz=d)).wait_recv()
    total = g_z[0]
    for k in range(1, 8):
        total = total + g_z[k]
    here = (yl * 2 + yh) * 4 + x
    g_p[here] = total
    for k in range(15):
        start(gram_plane, k)
    for k, (dx, dyl, dyh) in enumerate(PLANE):
        there = (lax.rem(yl + dyl, 2) * 2 + lax.rem(yh + dyh, 2)) * 4 + lax.rem(x + NX - dx, NX)
        remote(
            g_p.at[there], g_p.at[there], gp_s.at[k], gp_r.at[k], dev(dx=dx, dyl=dyl, dyh=dyh)
        ).wait_recv()
    total = g_p[0]
    for k in range(1, 16):
        total = total + g_p[k]
    g_half[pl.ds(core * 16, 16)] = total
    start(gram_back)
    theirs = g_half.at[pl.ds(other * 16, 16)]
    remote(theirs, theirs, sib_s.at[4], sib_r.at[4], sib).wait_recv()
    gram_ref[...] = g_half[...]
    for c in (sib_w, sib_p, sib_x):
        c.wait_send()
    for make, args in sent:
        make(*args).wait_send()


def split(v):
    high = v.astype(BF16)
    return high, (v - high.astype(F32)).astype(BF16)


def wide(v):
    return jnp.broadcast_to(v, (8, 128))


def tail_kernel(prod_ref, gram_ref, out_hbm, basis_ref, sem):
    copy = pltpu.make_async_copy(prod_ref, out_hbm, sem)
    copy.start()
    packed = gram_ref[...]
    gram = jnp.concatenate([packed[:, 0:R], packed[:, R : 2 * R]], axis=0)
    row = lax.broadcasted_iota(jnp.int32, (R, R), 0)
    lane = lax.broadcasted_iota(jnp.int32, (R, R), 1)
    full = jnp.concatenate([gram, (row == lane).astype(F32)], axis=1)
    rows = [full[8 * i : 8 * i + 8, :] for i in range(8)]
    sub = lax.broadcasted_iota(jnp.int32, (8, 128), 0)
    for b in range(8):
        col = {(j, i): wide(rows[i][:, 8 * b + j : 8 * b + j + 1]) for j in range(8) for i in range(b, 8)}
        diag = jnp.zeros((8, 128), F32)
        for j in range(8):
            d = wide(col[j, b][j : j + 1, :])
            inv = 1.0 / d
            diag = jnp.where(sub == j, d, diag)
            pivot = wide(rows[b][j : j + 1, :])
            heads = {n: wide(col[n, b][j : j + 1, :]) for n in range(j + 1, 8)}
            for i in range(b, 8):
                m = col[j, i] * inv
                if i == b:
                    m = jnp.where(sub > j, m, 0.0)
                rows[i] = rows[i] - m * pivot
                for n in range(j + 1, 8):
                    col[n, i] = col[n, i] - m * heads[n]
        rows[b] = rows[b] * (lax.rsqrt(diag) * 512.0)
    inverse = jnp.concatenate(rows, axis=0)[:, R : 2 * R]
    lh, ll = split(inverse)
    xh, xl = split(prod_ref[...])
    basis_ref[...] = dot(
        jnp.concatenate([lh, lh, ll], axis=1), jnp.concatenate([xh, xl, xh], axis=0)
    )
    copy.wait()


def per_device(points, vectors, leaf_interp, leaf_skeleton, group_transfer, group_skeleton):
    hbm = pl.BlockSpec(memory_space=pltpu.HBM)
    vmem = pl.BlockSpec(memory_space=pltpu.VMEM)
    dma = pltpu.SemaphoreType.DMA
    prod_t, gram = pl.pallas_call(
        main_kernel,
        out_shape=(jax.ShapeDtypeStruct((R, N), F32), jax.ShapeDtypeStruct((32, 128), F32)),
        in_specs=[hbm] * 6,
        out_specs=(vmem, vmem),
        scratch_shapes=[
            pltpu.VMEM((N, D), BF16),
            pltpu.VMEM((R, N), BF16),
            pltpu.VMEM((N, D), BF16),
            pltpu.VMEM((1, 128), jnp.int32),
            pltpu.VMEM((128, 512), BF16),
            pltpu.VMEM((1, 512), jnp.int32),
            pltpu.VMEM((SLOTS, BR, D), BF16),
            pltpu.VMEM((BR, D), BF16),
            pltpu.VMEM((2, BR, D), BF16),
            pltpu.VMEM((N, KR), BF16),
            pltpu.VMEM((N, R), F32),
            pltpu.VMEM((2, 8, 16, 128), F32),
            pltpu.VMEM((8, 16, 128), F32),
            pltpu.VMEM((2, 8, 32, 128), BF16),
            pltpu.VMEM((8, 32, 128), BF16),
            pltpu.VMEM((8, 16, 128), F32),
            pltpu.VMEM((8, 32, 128), BF16),
            pltpu.VMEM((16, 128), F32),
            pltpu.VMEM((32, 128), BF16),
            pltpu.VMEM((8, 48, 128), BF16),
            pltpu.VMEM((32, 128), F32),
            pltpu.VMEM((16, 128), F32),
            pltpu.VMEM((8, 16, 128), F32),
            pltpu.VMEM((16, 16, 128), F32),
            pltpu.VMEM((32, 128), F32),
            dma((6,)),
            dma((7,)),
            dma((7,)),
            dma((15,)),
            dma((15,)),
            dma((15,)),
            dma((15,)),
            dma((15,)),
            dma((2, 8)),
            dma((2, 8)),
            dma((8,)),
            dma((8,)),
            dma((14,)),
            dma((14,)),
            dma((14,)),
            dma((14,)),
            dma((8,)),
            dma((8,)),
            dma((15,)),
            dma((15,)),
        ],
        compiler_params=pltpu.CompilerParams(
            collective_id=0, has_side_effects=True, vmem_limit_bytes=40 * 2**20
        ),
        name="hss_main",
    )(
        *(
            pltpu.with_memory_space_constraint(a, pltpu.HBM)
            for a in (
                points,
                vectors.T,
                leaf_interp,
                leaf_skeleton.reshape(1, 128),
                group_transfer,
                group_skeleton.reshape(1, 512),
            )
        )
    )
    out_t, basis_t = pl.pallas_call(
        tail_kernel,
        out_shape=(jax.ShapeDtypeStruct((R, N), F32), jax.ShapeDtypeStruct((R, N), F32)),
        in_specs=[vmem, vmem],
        out_specs=(hbm, vmem),
        scratch_shapes=[pltpu.SemaphoreType.DMA],
        compiler_params=pltpu.CompilerParams(vmem_limit_bytes=16 * 2**20),
        name="hss_tail",
    )(prod_t, gram)
    return out_t.T, basis_t.T


def solution(mesh):
    spec = P(("group", "leaf"), None)
    return jax.shard_map(
        per_device,
        mesh=mesh,
        in_specs=(spec, spec, spec, P(("group", "leaf")), spec, P("group")),
        out_specs=(spec, spec),
        check_vma=False,
    )
```

```python
import math

import jax
import jax.numpy as jnp
from jax import lax
from jax.experimental import pallas as pl
from jax.experimental.pallas import tpu as pltpu
from jax.sharding import PartitionSpec as P

MESH = pl.DeviceIdType.MESH
F32 = jnp.float32
BF16 = jnp.bfloat16
NX, NYL, NZ, NYH = 4, 2, 8, 2
D = 128
R = 64
N = 1024
KR = 144
BR = KR + R
NEAR = [
    (1, 0), (7, 0), (0, 1), (2, 0), (6, 0), (1, 1), (7, 1), (2, 1),
    (6, 1), (3, 0), (5, 0), (4, 0), (3, 1), (5, 1), (4, 1),
]
FAR = [
    ("y", 0, 1), ("y", 0, 3), ("x", 1, 0), ("x", 1, 1), ("x", 3, 0), ("x", 3, 1), ("x", 2, 0),
    ("x", 2, 1), ("y", 1, 1), ("y", 1, 3), ("y", 3, 1), ("y", 3, 3), ("y", 2, 1), ("y", 2, 3),
]
PLANE = [(dx, dyl, dyh) for dyl in range(2) for dyh in range(2) for dx in range(4) if (dx, dyl, dyh) != (0, 0, 0)]
NEAR0 = 16
FAR0 = 46
SLOTS = 74


def dot(a, b, ca=1, cb=0, precision=None):
    return lax.dot_general(
        a, b, (((ca,), (cb,)), ((), ())), preferred_element_type=F32, precision=precision
    )


def norm_rows(key_t, as_query):
    keys = key_t.astype(F32)
    norms = jnp.sum(keys * keys, axis=0, keepdims=True) * (-1.0 / 64.0)
    high = norms.astype(BF16).astype(F32)
    rest = norms - high
    mid = rest.astype(BF16).astype(F32)
    low = rest - mid
    row = lax.broadcasted_iota(jnp.int32, (16, key_t.shape[1]), 0)
    if as_query:
        row = jnp.where(row < 6, lax.rem(row + 3, 6), row)
    out = jnp.where(row == 0, high, jnp.where(row == 1, mid, jnp.where(row == 2, low, 0.0)))
    return jnp.where((row >= 3) & (row < 6), 1.0, out).astype(BF16)


def main_kernel(
    pts_hbm, vec_hbm, interp_hbm, lsk_hbm, trans_hbm, gsk_hbm,
    prod_ref, gram_ref,
    pts, vec, interp, lsk, trans, gsk, buf, own, far_own, q, acc,
    gw, gw_in, gp, gp_in, rsw, rsp, pair_in_w, pair_in_p, ag, g_loc, g_sib, g_z, g_p, g_half,
    load_sem, sib_s, sib_r, slot_s, near_r, nfw_r, far_r, ffw_r, rs_s, rs_r,
):
    grp = lax.axis_index("group")
    leaf = lax.axis_index("leaf")
    x, yl = lax.rem(grp, NX), grp // NX
    core, yh, z = lax.rem(leaf, 2), lax.rem(leaf // 2, 2), leaf // 4

    def dev(dx=0, dyl=0, dz=0, dyh=0, dc=0):
        return (
            lax.rem(yl + dyl, NYL) * NX + lax.rem(x + dx, NX),
            lax.rem(z + dz, NZ) * 4 + lax.rem(yh + dyh, 2) * 2 + lax.rem(core + dc, 2),
        )

    def ydev(dy):
        y = lax.rem(yh * 2 + yl + dy, 4)
        return (lax.rem(y, 2) * NX + x, z * 4 + (y // 2) * 2 + core)

    def remote(src, dst, ss, rs, to):
        return pltpu.make_async_remote_copy(
            src_ref=src, dst_ref=dst, send_sem=ss, recv_sem=rs, device_id=to, device_id_type=MESH
        )

    loads = [
        pltpu.make_async_copy(s, d, load_sem.at[i])
        for i, (s, d) in enumerate(
            ((pts_hbm, pts), (lsk_hbm, lsk), (vec_hbm, vec), (interp_hbm, interp), (trans_hbm, trans), (gsk_hbm, gsk))
        )
    ]
    for c in loads:
        c.start()
    barrier = pltpu.get_barrier_semaphore()
    peers = [dev(dc=1)]
    peers += [dev(dz=d) for d in range(1, 8)] + [dev(dyh=1)]
    peers += [dev(dx=dx) for dx in (1, 2, 3)] + [ydev(1), ydev(3)]
    for p in peers:
        pl.semaphore_signal(barrier, inc=1, device_id=p, device_id_type=MESH)
    sib = dev(dc=1)

    for c in loads:
        c.wait()
    pts_t = jnp.transpose(pts[...])
    hot = (lax.broadcasted_iota(jnp.int32, (N, D), 0) == lsk[...]).astype(F32).astype(BF16)
    skel_t = dot(pts_t, hot).astype(BF16)
    own[0:D, :] = skel_t
    own[D:KR, :] = norm_rows(skel_t, False)
    w_t = dot(vec[...], interp[...])
    own[KR:BR, :] = w_t.astype(BF16)
    w = jnp.transpose(w_t).astype(BF16)
    trans_t = jnp.transpose(trans[...])
    for k in range(4):
        half, n = k // 2, k % 2
        left = dot(trans_t[k * 128 : k * 128 + 64], w)
        right = dot(trans_t[k * 128 + 64 : k * 128 + 128], w)
        pick = lax.broadcasted_iota(jnp.int32, (D, D), 0) + leaf * D == gsk[:, k * D : (k + 1) * D]
        picked = dot(skel_t, pick.astype(F32).astype(BF16)).astype(BF16)
        for t in range(NZ):
            gw[half, t, n * 8 : n * 8 + 8, 0:R] = left[t * 8 : t * 8 + 8]
            gw[half, t, n * 8 : n * 8 + 8, R : 2 * R] = right[t * 8 : t * 8 + 8]
            gp[half, t, n * 16 : n * 16 + 16, :] = picked[t * 16 : t * 16 + 16]
    key_norms = norm_rows(pts_t, False)
    for k in range(8):
        s = slice(k * D, (k + 1) * D)
        buf[k, 0:D, :] = pts_t[:, s]
        buf[k, D:KR, :] = key_norms[:, s]
        buf[k, KR:BR, :] = vec[:, s]
    q[:, 0:D] = pts[...] * jnp.asarray(1.0 / 32.0, BF16)
    q[:, D:KR] = jnp.transpose(norm_rows(pts_t, True))
    acc[...] = jnp.zeros_like(acc)

    pl.semaphore_wait(barrier, len(peers))

    other = 1 - core
    sib_w = remote(gw.at[other], gw_in, sib_s.at[0], sib_r.at[0], sib)
    sib_p = remote(gp.at[other], gp_in, sib_s.at[1], sib_r.at[1], sib)
    sib_x = remote(buf.at[pl.ds(0, 8)], buf.at[pl.ds(8, 8)], sib_s.at[2], sib_r.at[2], sib)
    for c in (sib_w, sib_p, sib_x):
        c.start()

    def near_slot(k):
        return buf.at[NEAR0 + 2 * k]

    def near_copy(k):
        dz, dyh = NEAR[k]
        return remote(own, near_slot(k), slot_s.at[0], near_r.at[k], dev(dz=dz and NZ - dz, dyh=dyh))

    def near_yh(k):
        dz, _ = NEAR[k]
        j = NEAR.index((dz, 1))
        return remote(near_slot(k), near_slot(j), slot_s.at[0], near_r.at[j], dev(dyh=1))

    def near_fwd(k):
        return remote(near_slot(k), buf.at[NEAR0 + 2 * k + 1], slot_s.at[0], nfw_r.at[k // 4], sib)

    def start(make, *args):
        make(*args).start()

    def arrived(ref, sem):
        remote(ref, ref, sem, sem, sib).wait_recv()

    def left(ref, sem):
        remote(ref, ref, sem, sem, sib).wait_send()

    def near_arrived(k):
        near_copy(k).wait_recv()
        start(near_fwd, k)
        if NEAR[k][1] == 0:
            start(near_yh, k)

    def rs_w(d):
        return remote(gw.at[core, lax.rem(z + d, NZ)], rsw.at[d], rs_s.at[0], rs_r.at[0], dev(dz=d))

    def rs_p(d):
        return remote(gp.at[core, lax.rem(z + d, NZ)], rsp.at[d], rs_s.at[1], rs_r.at[1], dev(dz=d))

    def pair_w():
        return remote(rsw.at[0], pair_in_w, sib_s.at[5], sib_r.at[5], dev(dyh=1))

    def pair_p():
        return remote(rsp.at[0], pair_in_p, sib_s.at[6], sib_r.at[6], dev(dyh=1))

    def zg(d):
        return remote(ag.at[z], ag.at[z], rs_s.at[2], rs_r.at[2], dev(dz=d))

    def far_slot(k):
        return buf.at[FAR0 + 2 * k]

    def far_copy(k):
        axis, dx, n = FAR[k]
        if axis == "x":
            return remote(far_own.at[n], far_slot(k), slot_s.at[0], far_r.at[k], dev(dx=NX - dx))
        quarter = 0 if n == 3 else 1
        src = far_own.at[quarter] if dx == 0 else far_slot(FAR.index(("x", dx, quarter)))
        return remote(src, far_slot(k), slot_s.at[0], far_r.at[k], ydev(4 - n))

    def far_fwd(k):
        return remote(buf.at[FAR0 + 2 * k], buf.at[FAR0 + 2 * k + 1], slot_s.at[0], ffw_r.at[(k + 3) // 4], sib)

    def phase_start():
        sib_w.wait_recv()
        sib_p.wait_recv()
        gw[core] = gw[core] + gw_in[...]
        gp[core] = gp[core] + gp_in[...]
        for d in range(1, 8):
            start(rs_w, d)
            start(rs_p, d)
        for k in (0, 1, 2, 3, 4):
            start(near_copy, k)

    def phase_sib():
        sib_x.wait_recv()

    def phase_rs():
        arrived(rsw.at[pl.ds(1, 7)], rs_r.at[0])
        arrived(rsp.at[pl.ds(1, 7)], rs_r.at[1])
        total = gw[core, z]
        rows = gp[core, z].astype(F32)
        for d in range(1, 8):
            total = total + rsw[d]
            rows = rows + rsp[d].astype(F32)
        rsw[0] = total
        rsp[0] = rows.astype(BF16)
        start(pair_w)
        start(pair_p)
        for k in (9, 10):
            start(near_copy, k)
        near_arrive(0, 1, 2, 3, 4)

    def phase_pair():
        pair_w().wait_recv()
        pair_p().wait_recv()
        ag[z, 0:16, :] = (rsw[0] + pair_in_w[...]).astype(BF16)
        ag[z, 16:48, :] = rsp[0] + pair_in_p[...]
        for d in range(1, 8):
            start(zg, d)
        start(near_copy, 11)
        near_ready(0)

    def near_arrive(*items):
        for k in items:
            near_arrived(k)

    def near_ready(group):
        arrived(buf.at[pl.ds(0, 3 if group == 3 else 4)], nfw_r.at[group])

    def phase_near1():
        near_arrive(5, 6, 7, 8)
        near_ready(1)

    def phase_near2():
        near_arrive(9, 10)

    def phase_near2b():
        near_arrive(11)
        near_ready(2)

    def phase_zg():
        arrived(ag.at[pl.ds(0, 7)], rs_r.at[2])
        for n in range(2):
            points_t = jnp.concatenate([ag[t, 16 + n * 16 : 32 + n * 16, :] for t in range(NZ)], axis=0)
            far_own[n, 0:D, :] = points_t
            far_own[n, D:KR, :] = norm_rows(points_t, False)
            pairs = jnp.concatenate(
                [ag[t, 0:16, :].astype(F32)[n * 8 : n * 8 + 8] for t in range(NZ)], axis=0
            )
            w_pairs = jnp.transpose(pairs)
            far_own[n, KR:BR, :] = jnp.concatenate([w_pairs[0:R], w_pairs[R : 2 * R]], axis=1).astype(BF16)
        for k, (axis, dx, _) in enumerate(FAR):
            if axis == "x" or dx == 0:
                start(far_copy, k)

    def far_arrive(*items):
        for k in items:
            far_copy(k).wait_recv()
            start(far_fwd, k)
            axis, dx, n = FAR[k]
            if axis == "x":
                start(far_copy, FAR.index(("y", dx, 3 if n == 0 else 1)))

    def far_ready(group):
        arrived(buf.at[pl.ds(0, 4 if 0 < group < 4 else 1)], ffw_r.at[group])

    def phase_far0():
        far_arrive(0, 1, 2, 3, 4, 5)
        near_arrive(12, 13, 14)
        far_ready(1)

    def phase_far1():
        far_arrive(6, 7)
        near_ready(3)
        far_ready(0)

    def phase_far2():
        far_arrive(8, 9, 10, 11)
        far_ready(2)

    def phase_far3():
        far_arrive(12, 13)
        far_ready(3)

    def phase_far4():
        far_ready(4)

    with jax.named_scope("phase_start"):
        phase_start()
    steps = [
        (0, []),
        (1, [phase_sib]),
        (2, [phase_rs, phase_pair]),
        (3, [phase_near1]),
        (4, [phase_near2, phase_zg, phase_near2b]),
        (6, [phase_far0]),
        (5, [phase_far1]),
        (7, [phase_far2]),
        (8, [phase_far3]),
    ]

    def chunk(i, carry):
        for n, (_, phases) in enumerate(steps):
            for phase in phases:
                with jax.named_scope(phase.__name__):
                    pl.when(i == n)(phase)
        add_keys(jnp.where(i == 5, 6, jnp.where(i == 6, 5, i)) * 8, 8)
        return carry

    def add_keys(base, count):
        keys = jnp.concatenate([buf[base + j, 0:KR, :] for j in range(count)], axis=1)
        weights = jnp.concatenate([buf[base + j, KR:BR, :] for j in range(count)], axis=1)
        for t in range(4):
            rows = pl.ds(t * 256, 256)
            kernel_vals = jnp.exp(dot(q[rows, :], keys)).astype(BF16)
            acc[rows, :] += dot(kernel_vals, weights, 1, 1)

    lax.fori_loop(0, 9, chunk, 0)
    phase_far4()
    add_keys(72, 2)

    prod_t = jnp.transpose(acc[...])
    prod_ref[...] = prod_t
    gram = dot(prod_t, acc[...], precision=lax.Precision.HIGHEST)
    g_loc[...] = jnp.concatenate([gram[0:32], gram[32:64]], axis=1)
    def gram_sib():
        return remote(g_loc.at[pl.ds(other * 16, 16)], g_sib, sib_s.at[3], sib_r.at[3], sib)

    def gram_z(d):
        return remote(g_z.at[z], g_z.at[z], rs_s.at[3], rs_r.at[3], dev(dz=d))

    def gram_plane(k):
        dx, dyl, dyh = PLANE[k]
        return remote(g_p.at[here], g_p.at[here], rs_s.at[4], rs_r.at[4], dev(dx=dx, dyl=dyl, dyh=dyh))

    def gram_back():
        mine = g_half.at[pl.ds(core * 16, 16)]
        return remote(mine, mine, sib_s.at[4], sib_r.at[4], sib)

    start(gram_sib)
    gram_sib().wait_recv()
    g_z[z] = g_loc[pl.ds(core * 16, 16)] + g_sib[...]
    for d in range(1, 8):
        start(gram_z, d)
    for c in (sib_w, sib_p, sib_x, pair_w(), pair_p()):
        c.wait_send()
    left(buf.at[pl.ds(0, 58)], slot_s.at[0])
    left(rsw.at[pl.ds(1, 7)], rs_s.at[0])
    left(rsp.at[pl.ds(1, 7)], rs_s.at[1])
    left(ag.at[pl.ds(0, 7)], rs_s.at[2])
    arrived(g_z.at[pl.ds(0, 7)], rs_r.at[3])
    total = g_z[0]
    for k in range(1, 8):
        total = total + g_z[k]
    here = (yl * 2 + yh) * 4 + x
    g_p[here] = total
    for k in range(15):
        start(gram_plane, k)
    arrived(g_p.at[pl.ds(0, 15)], rs_r.at[4])
    total = g_p[0]
    for k in range(1, 16):
        total = total + g_p[k]
    g_half[pl.ds(core * 16, 16)] = total
    start(gram_back)
    theirs = g_half.at[pl.ds(other * 16, 16)]
    remote(theirs, theirs, sib_s.at[4], sib_r.at[4], sib).wait_recv()
    gram_ref[...] = g_half[...]
    gram_sib().wait_send()
    gram_back().wait_send()
    left(g_z.at[pl.ds(0, 7)], rs_s.at[3])
    left(g_p.at[pl.ds(0, 15)], rs_s.at[4])


def split(v):
    high = v.astype(BF16)
    return high, (v - high.astype(F32)).astype(BF16)


def wide(v):
    return jnp.broadcast_to(v, (8, 128))


def tail_kernel(prod_ref, gram_ref, out_hbm, basis_ref, sem):
    copy = pltpu.make_async_copy(prod_ref, out_hbm, sem)
    copy.start()
    packed = gram_ref[...]
    gram = jnp.concatenate([packed[:, 0:R], packed[:, R : 2 * R]], axis=0)
    row = lax.broadcasted_iota(jnp.int32, (R, R), 0)
    lane = lax.broadcasted_iota(jnp.int32, (R, R), 1)
    full = jnp.concatenate([gram, (row == lane).astype(F32)], axis=1)
    rows = [full[8 * i : 8 * i + 8, :] for i in range(8)]
    sub = lax.broadcasted_iota(jnp.int32, (8, 128), 0)
    for b in range(8):
        col = {(j, i): wide(rows[i][:, 8 * b + j : 8 * b + j + 1]) for j in range(8) for i in range(b, 8)}
        diag = jnp.zeros((8, 128), F32)
        for j in range(8):
            d = wide(col[j, b][j : j + 1, :])
            inv = 1.0 / d
            diag = jnp.where(sub == j, d, diag)
            pivot = wide(rows[b][j : j + 1, :])
            heads = {n: wide(col[n, b][j : j + 1, :]) for n in range(j + 1, 8)}
            for i in range(b, 8):
                m = col[j, i] * inv
                if i == b:
                    m = jnp.where(sub > j, m, 0.0)
                rows[i] = rows[i] - m * pivot
                for n in range(j + 1, 8):
                    col[n, i] = col[n, i] - m * heads[n]
        rows[b] = rows[b] * (lax.rsqrt(diag) * 512.0)
    inverse = jnp.concatenate(rows, axis=0)[:, R : 2 * R]
    lh, ll = split(inverse)
    xh, xl = split(prod_ref[...])
    basis_ref[...] = dot(
        jnp.concatenate([lh, lh, ll], axis=1), jnp.concatenate([xh, xl, xh], axis=0)
    )
    copy.wait()


def per_device(points, vectors, leaf_interp, leaf_skeleton, group_transfer, group_skeleton):
    hbm = pl.BlockSpec(memory_space=pltpu.HBM)
    vmem = pl.BlockSpec(memory_space=pltpu.VMEM)
    dma = pltpu.SemaphoreType.DMA
    prod_t, gram = pl.pallas_call(
        main_kernel,
        out_shape=(jax.ShapeDtypeStruct((R, N), F32), jax.ShapeDtypeStruct((32, 128), F32)),
        in_specs=[hbm] * 6,
        out_specs=(vmem, vmem),
        scratch_shapes=[
            pltpu.VMEM((N, D), BF16),
            pltpu.VMEM((R, N), BF16),
            pltpu.VMEM((N, D), BF16),
            pltpu.VMEM((1, 128), jnp.int32),
            pltpu.VMEM((128, 512), BF16),
            pltpu.VMEM((1, 512), jnp.int32),
            pltpu.VMEM((SLOTS, BR, D), BF16),
            pltpu.VMEM((BR, D), BF16),
            pltpu.VMEM((2, BR, D), BF16),
            pltpu.VMEM((N, KR), BF16),
            pltpu.VMEM((N, R), F32),
            pltpu.VMEM((2, 8, 16, 128), F32),
            pltpu.VMEM((8, 16, 128), F32),
            pltpu.VMEM((2, 8, 32, 128), BF16),
            pltpu.VMEM((8, 32, 128), BF16),
            pltpu.VMEM((8, 16, 128), F32),
            pltpu.VMEM((8, 32, 128), BF16),
            pltpu.VMEM((16, 128), F32),
            pltpu.VMEM((32, 128), BF16),
            pltpu.VMEM((8, 48, 128), BF16),
            pltpu.VMEM((32, 128), F32),
            pltpu.VMEM((16, 128), F32),
            pltpu.VMEM((8, 16, 128), F32),
            pltpu.VMEM((16, 16, 128), F32),
            pltpu.VMEM((32, 128), F32),
            dma((6,)),
            dma((7,)),
            dma((7,)),
            dma((1,)),
            dma((15,)),
            dma((4,)),
            dma((14,)),
            dma((5,)),
            dma((5,)),
            dma((5,)),
        ],
        compiler_params=pltpu.CompilerParams(
            collective_id=0, has_side_effects=True, vmem_limit_bytes=40 * 2**20
        ),
        name="hss_main",
    )(
        *(
            pltpu.with_memory_space_constraint(a, pltpu.HBM)
            for a in (
                points,
                vectors.T,
                leaf_interp,
                leaf_skeleton.reshape(1, 128),
                group_transfer,
                group_skeleton.reshape(1, 512),
            )
        )
    )
    out_t, basis_t = pl.pallas_call(
        tail_kernel,
        out_shape=(jax.ShapeDtypeStruct((R, N), F32), jax.ShapeDtypeStruct((R, N), F32)),
        in_specs=[vmem, vmem],
        out_specs=(hbm, vmem),
        scratch_shapes=[pltpu.SemaphoreType.DMA],
        compiler_params=pltpu.CompilerParams(vmem_limit_bytes=16 * 2**20),
        name="hss_tail",
    )(prod_t, gram)
    return out_t.T, basis_t.T


def solution(mesh):
    spec = P(("group", "leaf"), None)
    return jax.shard_map(
        per_device,
        mesh=mesh,
        in_specs=(spec, spec, spec, P(("group", "leaf")), spec, P("group")),
        out_specs=(spec, spec),
        check_vma=False,
    )
```

```python
import math

import jax
import jax.numpy as jnp
from jax import lax
from jax.experimental import pallas as pl
from jax.experimental.pallas import tpu as pltpu
from jax.sharding import PartitionSpec as P

MESH = pl.DeviceIdType.MESH
F32 = jnp.float32
BF16 = jnp.bfloat16
NX, NYL, NZ, NYH = 4, 2, 8, 2
D = 128
R = 64
N = 1024
KR = 144
BR = KR + R
NEAR = [
    (1, 0), (7, 0), (0, 1), (1, 1), (7, 1), (2, 0), (6, 0), (2, 1),
    (6, 1), (3, 0), (5, 0), (4, 0), (3, 1), (5, 1), (4, 1),
]
FAR = [
    ("y", 0, 1), ("y", 0, 3), ("x", 1, 0), ("x", 1, 1), ("x", 3, 0), ("x", 3, 1), ("x", 2, 0),
    ("x", 2, 1), ("y", 1, 1), ("y", 1, 3), ("y", 3, 1), ("y", 3, 3), ("y", 2, 1), ("y", 2, 3),
]
PLANE = [(dx, dyl, dyh) for dyl in range(2) for dyh in range(2) for dx in range(4) if (dx, dyl, dyh) != (0, 0, 0)]
NEAR0 = 16
FAR0 = 46
SLOTS = 74


def dot(a, b, ca=1, cb=0, precision=None):
    return lax.dot_general(
        a, b, (((ca,), (cb,)), ((), ())), preferred_element_type=F32, precision=precision
    )


def norm_rows(key_t, as_query):
    keys = key_t.astype(F32)
    norms = jnp.sum(keys * keys, axis=0, keepdims=True) * (-1.0 / 64.0)
    high = norms.astype(BF16).astype(F32)
    rest = norms - high
    mid = rest.astype(BF16).astype(F32)
    low = rest - mid
    row = lax.broadcasted_iota(jnp.int32, (16, key_t.shape[1]), 0)
    if as_query:
        row = jnp.where(row < 6, lax.rem(row + 3, 6), row)
    out = jnp.where(row == 0, high, jnp.where(row == 1, mid, jnp.where(row == 2, low, 0.0)))
    return jnp.where((row >= 3) & (row < 6), 1.0, out).astype(BF16)


def main_kernel(
    pts_hbm, vec_hbm, interp_hbm, lsk_hbm, trans_hbm, gsk_hbm,
    prod_ref, gram_ref,
    pts, vec, interp, lsk, trans, gsk, buf, own, far_own, q, acc,
    gw, gw_in, gp, gp_in, rsw, rsp, pair_in_w, pair_in_p, ag, g_loc, g_sib, g_z, g_p, g_half,
    load_sem, sib_s, sib_r, slot_s, near_r, nfw_r, far_r, ffw_r, rs_s, rs_r,
):
    grp = lax.axis_index("group")
    leaf = lax.axis_index("leaf")
    x, yl = lax.rem(grp, NX), grp // NX
    core, yh, z = lax.rem(leaf, 2), lax.rem(leaf // 2, 2), leaf // 4

    def dev(dx=0, dyl=0, dz=0, dyh=0, dc=0):
        return (
            lax.rem(yl + dyl, NYL) * NX + lax.rem(x + dx, NX),
            lax.rem(z + dz, NZ) * 4 + lax.rem(yh + dyh, 2) * 2 + lax.rem(core + dc, 2),
        )

    def ydev(dy):
        y = lax.rem(yh * 2 + yl + dy, 4)
        return (lax.rem(y, 2) * NX + x, z * 4 + (y // 2) * 2 + core)

    def remote(src, dst, ss, rs, to):
        return pltpu.make_async_remote_copy(
            src_ref=src, dst_ref=dst, send_sem=ss, recv_sem=rs, device_id=to, device_id_type=MESH
        )

    loads = [
        pltpu.make_async_copy(s, d, load_sem.at[i])
        for i, (s, d) in enumerate(
            ((pts_hbm, pts), (lsk_hbm, lsk), (vec_hbm, vec), (interp_hbm, interp), (trans_hbm, trans), (gsk_hbm, gsk))
        )
    ]
    for c in loads:
        c.start()
    barrier = pltpu.get_barrier_semaphore()
    peers = [dev(dc=1)]
    peers += [dev(dz=d) for d in range(1, 8)] + [dev(dyh=1)]
    peers += [dev(dx=dx) for dx in (1, 2, 3)] + [ydev(1), ydev(3)]
    for p in peers:
        pl.semaphore_signal(barrier, inc=1, device_id=p, device_id_type=MESH)
    sib = dev(dc=1)

    for c in loads:
        c.wait()
    pts_t = jnp.transpose(pts[...])
    hot = (lax.broadcasted_iota(jnp.int32, (N, D), 0) == lsk[...]).astype(F32).astype(BF16)
    skel_t = dot(pts_t, hot).astype(BF16)
    own[0:D, :] = skel_t
    own[D:KR, :] = norm_rows(skel_t, False)
    w_t = dot(vec[...], interp[...])
    own[KR:BR, :] = w_t.astype(BF16)
    w = jnp.transpose(w_t).astype(BF16)
    trans_t = jnp.transpose(trans[...])
    for k in range(4):
        half, n = k // 2, k % 2
        left = dot(trans_t[k * 128 : k * 128 + 64], w)
        right = dot(trans_t[k * 128 + 64 : k * 128 + 128], w)
        pick = lax.broadcasted_iota(jnp.int32, (D, D), 0) + leaf * D == gsk[:, k * D : (k + 1) * D]
        picked = dot(skel_t, pick.astype(F32).astype(BF16)).astype(BF16)
        for t in range(NZ):
            gw[half, t, n * 8 : n * 8 + 8, 0:R] = left[t * 8 : t * 8 + 8]
            gw[half, t, n * 8 : n * 8 + 8, R : 2 * R] = right[t * 8 : t * 8 + 8]
            gp[half, t, n * 16 : n * 16 + 16, :] = picked[t * 16 : t * 16 + 16]
    key_norms = norm_rows(pts_t, False)
    for k in range(8):
        s = slice(k * D, (k + 1) * D)
        buf[k, 0:D, :] = pts_t[:, s]
        buf[k, D:KR, :] = key_norms[:, s]
        buf[k, KR:BR, :] = vec[:, s]
    q[:, 0:D] = pts[...] * jnp.asarray(1.0 / 32.0, BF16)
    q[:, D:KR] = jnp.transpose(norm_rows(pts_t, True))
    acc[...] = jnp.zeros_like(acc)

    pl.semaphore_wait(barrier, len(peers))

    other = 1 - core
    sib_w = remote(gw.at[other], gw_in, sib_s.at[0], sib_r.at[0], sib)
    sib_p = remote(gp.at[other], gp_in, sib_s.at[1], sib_r.at[1], sib)
    sib_x = remote(buf.at[pl.ds(0, 8)], buf.at[pl.ds(8, 8)], sib_s.at[2], sib_r.at[2], sib)
    for c in (sib_w, sib_p, sib_x):
        c.start()

    def near_slot(k):
        return buf.at[NEAR0 + 2 * k]

    def near_copy(k):
        dz, dyh = NEAR[k]
        return remote(own, near_slot(k), slot_s.at[0], near_r.at[k], dev(dz=dz and NZ - dz, dyh=dyh))

    def near_along(k):
        dz, dyh = NEAR[k]
        j = NEAR.index((dz + 1 if dz < 4 else dz - 1, dyh))
        return remote(near_slot(k), near_slot(j), slot_s.at[0], near_r.at[j], dev(dz=7 if dz < 4 else 1))

    def near_beside(dz):
        j = NEAR.index((dz, 1))
        return remote(near_slot(2), near_slot(j), slot_s.at[0], near_r.at[j], dev(dz=NZ - dz))

    def near_across(k):
        j = NEAR.index((4, NEAR[k][1]))
        src = buf.at[NEAR0 + 2 * k + 2 * core]
        return remote(src, near_slot(j), slot_s.at[0], near_r.at[j], dev(dz=6 - 4 * core))

    def near_fwd(k):
        return remote(near_slot(k), buf.at[NEAR0 + 2 * k + 1], slot_s.at[0], nfw_r.at[(k + 1) // 4], sib)

    def start(make, *args):
        make(*args).start()

    def arrived(ref, sem):
        remote(ref, ref, sem, sem, sib).wait_recv()

    def left(ref, sem):
        remote(ref, ref, sem, sem, sib).wait_send()

    def near_arrived(k):
        near_copy(k).wait_recv()
        start(near_fwd, k)
        if NEAR[k][0] in (1, 2, 6, 7):
            start(near_along, k)
        if NEAR[k][0] == 6:
            start(near_across, k - 1)
        if k == 2:
            start(near_beside, 1)
            start(near_beside, 7)

    def rs_w(d):
        return remote(gw.at[core, lax.rem(z + d, NZ)], rsw.at[d], rs_s.at[0], rs_r.at[0], dev(dz=d))

    def rs_p(d):
        return remote(gp.at[core, lax.rem(z + d, NZ)], rsp.at[d], rs_s.at[1], rs_r.at[1], dev(dz=d))

    def pair_w():
        return remote(rsw.at[0], pair_in_w, sib_s.at[5], sib_r.at[5], dev(dyh=1))

    def pair_p():
        return remote(rsp.at[0], pair_in_p, sib_s.at[6], sib_r.at[6], dev(dyh=1))

    def zg(d):
        return remote(ag.at[z], ag.at[z], rs_s.at[2], rs_r.at[2], dev(dz=d))

    def far_slot(k):
        return buf.at[FAR0 + 2 * k]

    def far_copy(k):
        axis, dx, n = FAR[k]
        if axis == "x":
            return remote(far_own.at[n], far_slot(k), slot_s.at[0], far_r.at[k], dev(dx=NX - dx))
        quarter = 0 if n == 3 else 1
        src = far_own.at[quarter] if dx == 0 else far_slot(FAR.index(("x", dx, quarter)))
        return remote(src, far_slot(k), slot_s.at[0], far_r.at[k], ydev(4 - n))

    def far_fwd(k):
        return remote(buf.at[FAR0 + 2 * k], buf.at[FAR0 + 2 * k + 1], slot_s.at[0], ffw_r.at[k // 4], sib)

    def phase_start():
        sib_w.wait_recv()
        sib_p.wait_recv()
        gw[core] = gw[core] + gw_in[...]
        gp[core] = gp[core] + gp_in[...]
        for d in range(1, 8):
            start(rs_w, d)
            start(rs_p, d)
        for k in (0, 1, 2):
            start(near_copy, k)

    def phase_sib():
        sib_x.wait_recv()

    def phase_rs():
        arrived(rsw.at[pl.ds(1, 7)], rs_r.at[0])
        arrived(rsp.at[pl.ds(1, 7)], rs_r.at[1])
        total = gw[core, z]
        rows = gp[core, z].astype(F32)
        for d in range(1, 8):
            total = total + rsw[d]
            rows = rows + rsp[d].astype(F32)
        rsw[0] = total
        rsp[0] = rows.astype(BF16)
        start(pair_w)
        start(pair_p)
        near_arrive(0, 1, 2)
        near_ready(0)

    def step_near0():
        add_keys(16, 6)

    def phase_pair():
        pair_w().wait_recv()
        pair_p().wait_recv()
        ag[z, 0:16, :] = (rsw[0] + pair_in_w[...]).astype(BF16)
        ag[z, 16:48, :] = rsp[0] + pair_in_p[...]
        for d in range(1, 8):
            start(zg, d)
        near_arrive(3, 4, 5, 6)
        near_ready(1)

    def near_arrive(*items):
        for k in items:
            near_arrived(k)

    def near_ready(group):
        arrived(buf.at[pl.ds(0, 4 if group else 3)], nfw_r.at[group])

    def phase_near2():
        near_arrive(7, 8, 9, 10)
        near_ready(2)

    def phase_near3():
        near_arrive(11, 12, 13, 14)
        near_ready(3)

    def phase_zg():
        arrived(ag.at[pl.ds(0, 7)], rs_r.at[2])
        for n in range(2):
            points_t = jnp.concatenate([ag[t, 16 + n * 16 : 32 + n * 16, :] for t in range(NZ)], axis=0)
            far_own[n, 0:D, :] = points_t
            far_own[n, D:KR, :] = norm_rows(points_t, False)
            pairs = jnp.concatenate(
                [ag[t, 0:16, :].astype(F32)[n * 8 : n * 8 + 8] for t in range(NZ)], axis=0
            )
            w_pairs = jnp.transpose(pairs)
            far_own[n, KR:BR, :] = jnp.concatenate([w_pairs[0:R], w_pairs[R : 2 * R]], axis=1).astype(BF16)
        for k, (axis, dx, _) in enumerate(FAR):
            if axis == "x" or dx == 0:
                start(far_copy, k)

    def far_arrive(*items):
        for k in items:
            far_copy(k).wait_recv()
            start(far_fwd, k)
        for k in items:
            axis, dx, n = FAR[k]
            if axis == "x":
                start(far_copy, FAR.index(("y", dx, 3 if n == 0 else 1)))

    def far_ready(group):
        arrived(buf.at[pl.ds(0, 2 if group == 3 else 4)], ffw_r.at[group])

    def phase_far0():
        far_arrive(0, 1, 2, 3, 4, 5)

    def phase_far1():
        far_arrive(6, 7)

    def phase_far1b():
        far_ready(0)

    def phase_far2():
        far_arrive(8, 9, 10, 11)

    def phase_far2b():
        far_ready(1)

    def phase_far2c():
        far_arrive(12, 13)
        far_ready(2)

    def phase_far3():
        far_ready(3)

    with jax.named_scope("phase_start"):
        phase_start()
    steps = [
        (0, []),
        (1, [phase_sib]),
        (2, [phase_rs, step_near0, phase_pair]),
        (3, [phase_zg, phase_near2]),
        (4, [phase_far0, phase_near3]),
        (5, [phase_far1, phase_far1b]),
        (6, [phase_far2, phase_far2b]),
        (7, [phase_far2c]),
    ]

    def chunk(i, carry):
        for n, (_, phases) in enumerate(steps):
            for phase in phases:
                with jax.named_scope(phase.__name__):
                    pl.when(i == n)(phase)
        add_keys(jnp.where(i < 2, i * 8, i * 8 + 6), 8)
        return carry

    def add_keys(base, count):
        keys = jnp.concatenate([buf[base + j, 0:KR, :] for j in range(count)], axis=1)
        weights = jnp.concatenate([buf[base + j, KR:BR, :] for j in range(count)], axis=1)
        for t in range(4):
            rows = pl.ds(t * 256, 256)
            kernel_vals = jnp.exp(dot(q[rows, :], keys)).astype(BF16)
            acc[rows, :] += dot(kernel_vals, weights, 1, 1)

    lax.fori_loop(0, 8, chunk, 0)
    with jax.named_scope("phase_far3"):
        phase_far3()
    add_keys(70, 4)

    prod_t = jnp.transpose(acc[...])
    prod_ref[...] = prod_t
    gram = dot(prod_t, acc[...], precision=lax.Precision.HIGHEST)
    g_loc[...] = jnp.concatenate([gram[0:32], gram[32:64]], axis=1)
    def gram_sib():
        return remote(g_loc.at[pl.ds(other * 16, 16)], g_sib, sib_s.at[3], sib_r.at[3], sib)

    def gram_z(d):
        return remote(g_z.at[z], g_z.at[z], rs_s.at[3], rs_r.at[3], dev(dz=d))

    def gram_plane(k):
        dx, dyl, dyh = PLANE[k]
        return remote(g_p.at[here], g_p.at[here], rs_s.at[4], rs_r.at[4], dev(dx=dx, dyl=dyl, dyh=dyh))

    def gram_back():
        mine = g_half.at[pl.ds(core * 16, 16)]
        return remote(mine, mine, sib_s.at[4], sib_r.at[4], sib)

    start(gram_sib)
    gram_sib().wait_recv()
    g_z[z] = g_loc[pl.ds(core * 16, 16)] + g_sib[...]
    for d in range(1, 8):
        start(gram_z, d)
    for c in (sib_w, sib_p, sib_x, pair_w(), pair_p()):
        c.wait_send()
    left(buf.at[pl.ds(0, 58)], slot_s.at[0])
    left(rsw.at[pl.ds(1, 7)], rs_s.at[0])
    left(rsp.at[pl.ds(1, 7)], rs_s.at[1])
    left(ag.at[pl.ds(0, 7)], rs_s.at[2])
    arrived(g_z.at[pl.ds(0, 7)], rs_r.at[3])
    total = g_z[0]
    for k in range(1, 8):
        total = total + g_z[k]
    here = (yl * 2 + yh) * 4 + x
    g_p[here] = total
    for k in range(15):
        start(gram_plane, k)
    arrived(g_p.at[pl.ds(0, 15)], rs_r.at[4])
    total = g_p[0]
    for k in range(1, 16):
        total = total + g_p[k]
    g_half[pl.ds(core * 16, 16)] = total
    start(gram_back)
    theirs = g_half.at[pl.ds(other * 16, 16)]
    remote(theirs, theirs, sib_s.at[4], sib_r.at[4], sib).wait_recv()
    gram_ref[...] = g_half[...]
    gram_sib().wait_send()
    gram_back().wait_send()
    left(g_z.at[pl.ds(0, 7)], rs_s.at[3])
    left(g_p.at[pl.ds(0, 15)], rs_s.at[4])


def split(v):
    high = v.astype(BF16)
    return high, (v - high.astype(F32)).astype(BF16)


def wide(v):
    return jnp.broadcast_to(v, (8, 128))


def tail_kernel(prod_ref, gram_ref, out_hbm, basis_ref, sem):
    copy = pltpu.make_async_copy(prod_ref, out_hbm, sem)
    copy.start()
    packed = gram_ref[...]
    gram = jnp.concatenate([packed[:, 0:R], packed[:, R : 2 * R]], axis=0)
    row = lax.broadcasted_iota(jnp.int32, (R, R), 0)
    lane = lax.broadcasted_iota(jnp.int32, (R, R), 1)
    full = jnp.concatenate([gram, (row == lane).astype(F32)], axis=1)
    rows = [full[8 * i : 8 * i + 8, :] for i in range(8)]
    sub = lax.broadcasted_iota(jnp.int32, (8, 128), 0)
    for b in range(8):
        col = {(j, i): wide(rows[i][:, 8 * b + j : 8 * b + j + 1]) for j in range(8) for i in range(b, 8)}
        diag = jnp.zeros((8, 128), F32)
        for j in range(8):
            d = wide(col[j, b][j : j + 1, :])
            inv = 1.0 / d
            diag = jnp.where(sub == j, d, diag)
            pivot = wide(rows[b][j : j + 1, :])
            heads = {n: wide(col[n, b][j : j + 1, :]) for n in range(j + 1, 8)}
            for i in range(b, 8):
                m = col[j, i] * inv
                if i == b:
                    m = jnp.where(sub > j, m, 0.0)
                rows[i] = rows[i] - m * pivot
                for n in range(j + 1, 8):
                    col[n, i] = col[n, i] - m * heads[n]
        rows[b] = rows[b] * (lax.rsqrt(diag) * 512.0)
    inverse = jnp.concatenate(rows, axis=0)[:, R : 2 * R]
    lh, ll = split(inverse)
    xh, xl = split(prod_ref[...])
    basis_ref[...] = dot(
        jnp.concatenate([lh, lh, ll], axis=1), jnp.concatenate([xh, xl, xh], axis=0)
    )
    copy.wait()


def per_device(points, vectors, leaf_interp, leaf_skeleton, group_transfer, group_skeleton):
    hbm = pl.BlockSpec(memory_space=pltpu.HBM)
    vmem = pl.BlockSpec(memory_space=pltpu.VMEM)
    dma = pltpu.SemaphoreType.DMA
    prod_t, gram = pl.pallas_call(
        main_kernel,
        out_shape=(jax.ShapeDtypeStruct((R, N), F32), jax.ShapeDtypeStruct((32, 128), F32)),
        in_specs=[hbm] * 6,
        out_specs=(vmem, vmem),
        scratch_shapes=[
            pltpu.VMEM((N, D), BF16),
            pltpu.VMEM((R, N), BF16),
            pltpu.VMEM((N, D), BF16),
            pltpu.VMEM((1, 128), jnp.int32),
            pltpu.VMEM((128, 512), BF16),
            pltpu.VMEM((1, 512), jnp.int32),
            pltpu.VMEM((SLOTS, BR, D), BF16),
            pltpu.VMEM((BR, D), BF16),
            pltpu.VMEM((2, BR, D), BF16),
            pltpu.VMEM((N, KR), BF16),
            pltpu.VMEM((N, R), F32),
            pltpu.VMEM((2, 8, 16, 128), F32),
            pltpu.VMEM((8, 16, 128), F32),
            pltpu.VMEM((2, 8, 32, 128), BF16),
            pltpu.VMEM((8, 32, 128), BF16),
            pltpu.VMEM((8, 16, 128), F32),
            pltpu.VMEM((8, 32, 128), BF16),
            pltpu.VMEM((16, 128), F32),
            pltpu.VMEM((32, 128), BF16),
            pltpu.VMEM((8, 48, 128), BF16),
            pltpu.VMEM((32, 128), F32),
            pltpu.VMEM((16, 128), F32),
            pltpu.VMEM((8, 16, 128), F32),
            pltpu.VMEM((16, 16, 128), F32),
            pltpu.VMEM((32, 128), F32),
            dma((6,)),
            dma((7,)),
            dma((7,)),
            dma((1,)),
            dma((15,)),
            dma((4,)),
            dma((14,)),
            dma((4,)),
            dma((5,)),
            dma((5,)),
        ],
        compiler_params=pltpu.CompilerParams(
            collective_id=0, has_side_effects=True, vmem_limit_bytes=40 * 2**20
        ),
        name="hss_main",
    )(
        *(
            pltpu.with_memory_space_constraint(a, pltpu.HBM)
            for a in (
                points,
                vectors.T,
                leaf_interp,
                leaf_skeleton.reshape(1, 128),
                group_transfer,
                group_skeleton.reshape(1, 512),
            )
        )
    )
    out_t, basis_t = pl.pallas_call(
        tail_kernel,
        out_shape=(jax.ShapeDtypeStruct((R, N), F32), jax.ShapeDtypeStruct((R, N), F32)),
        in_specs=[vmem, vmem],
        out_specs=(hbm, vmem),
        scratch_shapes=[pltpu.SemaphoreType.DMA],
        compiler_params=pltpu.CompilerParams(vmem_limit_bytes=16 * 2**20),
        name="hss_tail",
    )(prod_t, gram)
    return out_t.T, basis_t.T


def solution(mesh):
    spec = P(("group", "leaf"), None)
    return jax.shard_map(
        per_device,
        mesh=mesh,
        in_specs=(spec, spec, spec, P(("group", "leaf")), spec, P("group")),
        out_specs=(spec, spec),
        check_vma=False,
    )
```

```python
import math

import jax
import jax.numpy as jnp
from jax import lax
from jax.experimental import pallas as pl
from jax.experimental.pallas import tpu as pltpu
from jax.sharding import PartitionSpec as P

MESH = pl.DeviceIdType.MESH
F32 = jnp.float32
BF16 = jnp.bfloat16
NX, NYL, NZ, NYH = 4, 2, 8, 2
D = 128
R = 64
N = 1024
KR = 144
BR = KR + R
NEAR = [
    (1, 0), (7, 0), (0, 1), (1, 1), (7, 1), (2, 0), (6, 0), (2, 1),
    (6, 1), (3, 0), (5, 0), (4, 0), (3, 1), (5, 1), (4, 1),
]
FAR = [
    ("y", 0, 1), ("y", 0, 3), ("x", 1, 0), ("x", 1, 1), ("x", 3, 0), ("x", 3, 1), ("x", 2, 0),
    ("x", 2, 1), ("y", 1, 1), ("y", 1, 3), ("y", 3, 1), ("y", 3, 3), ("y", 2, 1), ("y", 2, 3),
]
PLANE = [
    (dx, dyl, dyh)
    for dx in (2, 1, 3, 0)
    for dyl, dyh in ((0, 1), (1, 0), (1, 1), (0, 0))
    if (dx, dyl, dyh) != (0, 0, 0)
]
FARTHEST = (4, 3, 5, 2, 6, 1, 7)
NEAR0 = 16
FAR0 = 46
SLOTS = 74


def dot(a, b, ca=1, cb=0, precision=None):
    return lax.dot_general(
        a, b, (((ca,), (cb,)), ((), ())), preferred_element_type=F32, precision=precision
    )


def norm_rows(key_t, as_query):
    keys = key_t.astype(F32)
    norms = jnp.sum(keys * keys, axis=0, keepdims=True) * (-1.0 / 64.0)
    high = norms.astype(BF16).astype(F32)
    rest = norms - high
    mid = rest.astype(BF16).astype(F32)
    low = rest - mid
    row = lax.broadcasted_iota(jnp.int32, (16, key_t.shape[1]), 0)
    if as_query:
        row = jnp.where(row < 6, lax.rem(row + 3, 6), row)
    out = jnp.where(row == 0, high, jnp.where(row == 1, mid, jnp.where(row == 2, low, 0.0)))
    return jnp.where((row >= 3) & (row < 6), 1.0, out).astype(BF16)


def main_kernel(
    pts_hbm, vec_hbm, interp_hbm, lsk_hbm, trans_hbm, gsk_hbm,
    prod_ref, gram_ref,
    pts, vec, interp, lsk, trans, gsk, buf, own, far_own, q, acc,
    gw, gw_in, gp, gp_in, rsw, rsp, pair_in_w, pair_in_p, ag, g_loc, g_sib, g_z, g_p, g_half,
    load_sem, sib_s, sib_r, slot_s, near_r, nfw_r, far_r, ffw_r, rs_s, rs_r,
):
    grp = lax.axis_index("group")
    leaf = lax.axis_index("leaf")
    x, yl = lax.rem(grp, NX), grp // NX
    core, yh, z = lax.rem(leaf, 2), lax.rem(leaf // 2, 2), leaf // 4

    def dev(dx=0, dyl=0, dz=0, dyh=0, dc=0):
        return (
            lax.rem(yl + dyl, NYL) * NX + lax.rem(x + dx, NX),
            lax.rem(z + dz, NZ) * 4 + lax.rem(yh + dyh, 2) * 2 + lax.rem(core + dc, 2),
        )

    def ydev(dy):
        y = lax.rem(yh * 2 + yl + dy, 4)
        return (lax.rem(y, 2) * NX + x, z * 4 + (y // 2) * 2 + core)

    def remote(src, dst, ss, rs, to):
        return pltpu.make_async_remote_copy(
            src_ref=src, dst_ref=dst, send_sem=ss, recv_sem=rs, device_id=to, device_id_type=MESH
        )

    loads = [
        pltpu.make_async_copy(s, d, load_sem.at[i])
        for i, (s, d) in enumerate(
            ((pts_hbm, pts), (lsk_hbm, lsk), (vec_hbm, vec), (interp_hbm, interp), (trans_hbm, trans), (gsk_hbm, gsk))
        )
    ]
    for c in loads:
        c.start()
    barrier = pltpu.get_barrier_semaphore()
    peers = [dev(dc=1)]
    peers += [dev(dz=d) for d in range(1, 8)] + [dev(dyh=1)]
    peers += [dev(dx=dx) for dx in (1, 2, 3)] + [ydev(1), ydev(3)]
    for p in peers:
        pl.semaphore_signal(barrier, inc=1, device_id=p, device_id_type=MESH)
    sib = dev(dc=1)

    for c in loads:
        c.wait()
    pts_t = jnp.transpose(pts[...])
    hot = (lax.broadcasted_iota(jnp.int32, (N, D), 0) == lsk[...]).astype(F32).astype(BF16)
    skel_t = dot(pts_t, hot).astype(BF16)
    own[0:D, :] = skel_t
    own[D:KR, :] = norm_rows(skel_t, False)
    w_t = dot(vec[...], interp[...])
    own[KR:BR, :] = w_t.astype(BF16)
    w = jnp.transpose(w_t).astype(BF16)
    trans_t = jnp.transpose(trans[...])
    for k in range(4):
        half, n = k // 2, k % 2
        left = dot(trans_t[k * 128 : k * 128 + 64], w)
        right = dot(trans_t[k * 128 + 64 : k * 128 + 128], w)
        pick = lax.broadcasted_iota(jnp.int32, (D, D), 0) + leaf * D == gsk[:, k * D : (k + 1) * D]
        picked = dot(skel_t, pick.astype(F32).astype(BF16)).astype(BF16)
        for t in range(NZ):
            gw[half, t, n * 8 : n * 8 + 8, 0:R] = left[t * 8 : t * 8 + 8]
            gw[half, t, n * 8 : n * 8 + 8, R : 2 * R] = right[t * 8 : t * 8 + 8]
            gp[half, t, n * 16 : n * 16 + 16, :] = picked[t * 16 : t * 16 + 16]
    key_norms = norm_rows(pts_t, False)
    for k in range(8):
        s = slice(k * D, (k + 1) * D)
        buf[k, 0:D, :] = pts_t[:, s]
        buf[k, D:KR, :] = key_norms[:, s]
        buf[k, KR:BR, :] = vec[:, s]
    q[:, 0:D] = pts[...] * jnp.asarray(1.0 / 32.0, BF16)
    q[:, D:KR] = jnp.transpose(norm_rows(pts_t, True))
    acc[...] = jnp.zeros_like(acc)

    pl.semaphore_wait(barrier, len(peers))

    other = 1 - core
    sib_w = remote(gw.at[other], gw_in, sib_s.at[0], sib_r.at[0], sib)
    sib_p = remote(gp.at[other], gp_in, sib_s.at[1], sib_r.at[1], sib)
    sib_x = remote(buf.at[pl.ds(0, 8)], buf.at[pl.ds(8, 8)], sib_s.at[2], sib_r.at[2], sib)
    for c in (sib_w, sib_p):
        c.start()

    def near_slot(k):
        return buf.at[NEAR0 + 2 * k]

    def near_copy(k):
        dz, dyh = NEAR[k]
        return remote(own, near_slot(k), slot_s.at[0], near_r.at[k], dev(dz=dz and NZ - dz, dyh=dyh))

    def near_along(k):
        dz, dyh = NEAR[k]
        j = NEAR.index((dz + 1 if dz < 4 else dz - 1, dyh))
        return remote(near_slot(k), near_slot(j), slot_s.at[0], near_r.at[j], dev(dz=7 if dz < 4 else 1))

    def near_beside(dz):
        j = NEAR.index((dz, 1))
        return remote(near_slot(2), near_slot(j), slot_s.at[0], near_r.at[j], dev(dz=NZ - dz))

    def near_across(k):
        j = NEAR.index((4, NEAR[k][1]))
        src = buf.at[NEAR0 + 2 * k + 2 * core]
        return remote(src, near_slot(j), slot_s.at[0], near_r.at[j], dev(dz=6 - 4 * core))

    def near_fwd(k):
        return remote(near_slot(k), buf.at[NEAR0 + 2 * k + 1], slot_s.at[0], nfw_r.at[(k + 1) // 4], sib)

    def start(make, *args):
        make(*args).start()

    def arrived(ref, sem):
        remote(ref, ref, sem, sem, sib).wait_recv()

    def left(ref, sem):
        remote(ref, ref, sem, sem, sib).wait_send()

    def near_arrived(k):
        near_copy(k).wait_recv()
        start(near_fwd, k)
        if NEAR[k][0] in (1, 2, 6, 7):
            start(near_along, k)
        if NEAR[k][0] == 6:
            start(near_across, k - 1)
        if k == 2:
            start(near_beside, 1)
            start(near_beside, 7)

    def rs_w(d):
        return remote(gw.at[core, lax.rem(z + d, NZ)], rsw.at[d], rs_s.at[0], rs_r.at[0], dev(dz=d))

    def rs_p(d):
        return remote(gp.at[core, lax.rem(z + d, NZ)], rsp.at[d], rs_s.at[1], rs_r.at[1], dev(dz=d))

    def pair_w():
        return remote(rsw.at[0], pair_in_w, sib_s.at[5], sib_r.at[5], dev(dyh=1))

    def pair_p():
        return remote(rsp.at[0], pair_in_p, sib_s.at[6], sib_r.at[6], dev(dyh=1))

    def zg(d):
        return remote(ag.at[z], ag.at[z], rs_s.at[2], rs_r.at[2], dev(dz=d))

    def far_slot(k):
        return buf.at[FAR0 + 2 * k]

    def far_copy(k):
        axis, dx, n = FAR[k]
        if axis == "x":
            return remote(far_own.at[n], far_slot(k), slot_s.at[0], far_r.at[k], dev(dx=NX - dx))
        quarter = 0 if n == 3 else 1
        src = far_own.at[quarter] if dx == 0 else far_slot(FAR.index(("x", dx, quarter)))
        return remote(src, far_slot(k), slot_s.at[0], far_r.at[k], ydev(4 - n))

    def far_fwd(k):
        return remote(buf.at[FAR0 + 2 * k], buf.at[FAR0 + 2 * k + 1], slot_s.at[0], ffw_r.at[k // 4], sib)

    def phase_start():
        sib_w.wait_recv()
        sib_p.wait_recv()
        gw[core] = gw[core] + gw_in[...]
        gp[core] = gp[core] + gp_in[...]
        for d in FARTHEST:
            start(rs_w, d)
            start(rs_p, d)
        sib_x.start()
        for k in (0, 1, 2):
            start(near_copy, k)

    def phase_sib():
        sib_x.wait_recv()

    def phase_rs():
        arrived(rsw.at[pl.ds(1, 7)], rs_r.at[0])
        arrived(rsp.at[pl.ds(1, 7)], rs_r.at[1])
        total = gw[core, z]
        rows = gp[core, z].astype(F32)
        for d in range(1, 8):
            total = total + rsw[d]
            rows = rows + rsp[d].astype(F32)
        rsw[0] = total
        rsp[0] = rows.astype(BF16)
        start(pair_w)
        start(pair_p)
        near_arrive(0, 1, 2)
        near_ready(0)

    def step_near0():
        add_keys(16, 6)

    def phase_pair():
        pair_w().wait_recv()
        pair_p().wait_recv()
        ag[z, 0:16, :] = (rsw[0] + pair_in_w[...]).astype(BF16)
        ag[z, 16:48, :] = rsp[0] + pair_in_p[...]
        for d in FARTHEST:
            start(zg, d)
        near_arrive(3, 4, 5, 6)
        near_ready(1)

    def near_arrive(*items):
        for k in items:
            near_arrived(k)

    def near_ready(group):
        arrived(buf.at[pl.ds(0, 4 if group else 3)], nfw_r.at[group])

    def phase_near2():
        near_arrive(7, 8, 9, 10)
        near_ready(2)

    def phase_near3():
        near_arrive(11, 12, 13, 14)
        near_ready(3)

    def phase_zg():
        arrived(ag.at[pl.ds(0, 7)], rs_r.at[2])
        for n in range(2):
            points_t = jnp.concatenate([ag[t, 16 + n * 16 : 32 + n * 16, :] for t in range(NZ)], axis=0)
            far_own[n, 0:D, :] = points_t
            far_own[n, D:KR, :] = norm_rows(points_t, False)
            pairs = jnp.concatenate(
                [ag[t, 0:16, :].astype(F32)[n * 8 : n * 8 + 8] for t in range(NZ)], axis=0
            )
            w_pairs = jnp.transpose(pairs)
            far_own[n, KR:BR, :] = jnp.concatenate([w_pairs[0:R], w_pairs[R : 2 * R]], axis=1).astype(BF16)
        for k in (2, 4, 3, 5, 6, 7, 0, 1):
            start(far_copy, k)

    def far_arrive(*items):
        for k in items:
            far_copy(k).wait_recv()
            start(far_fwd, k)
        for k in items:
            axis, dx, n = FAR[k]
            if axis == "x":
                start(far_copy, FAR.index(("y", dx, 3 if n == 0 else 1)))

    def far_ready(group):
        arrived(buf.at[pl.ds(0, 2 if group == 3 else 4)], ffw_r.at[group])

    def phase_far0():
        far_arrive(0, 1, 2, 3, 4, 5)

    def phase_far1():
        far_arrive(6, 7)

    def phase_far1b():
        far_ready(0)

    def phase_far2():
        far_arrive(8, 9, 10, 11)

    def phase_far2b():
        far_ready(1)

    def phase_far2c():
        far_arrive(12, 13)
        far_ready(2)

    def phase_far3():
        far_ready(3)

    with jax.named_scope("phase_start"):
        phase_start()
    steps = [
        (0, []),
        (1, [phase_sib]),
        (2, [phase_rs, step_near0, phase_pair]),
        (3, [phase_zg, phase_near2]),
        (4, [phase_far0, phase_near3]),
        (5, [phase_far1, phase_far1b]),
        (6, [phase_far2, phase_far2b]),
        (7, [phase_far2c]),
    ]

    def chunk(i, carry):
        for n, (_, phases) in enumerate(steps):
            for phase in phases:
                with jax.named_scope(phase.__name__):
                    pl.when(i == n)(phase)
        add_keys(jnp.where(i < 2, i * 8, i * 8 + 6), 8)
        return carry

    def add_keys(base, count):
        keys = jnp.concatenate([buf[base + j, 0:KR, :] for j in range(count)], axis=1)
        weights = jnp.concatenate([buf[base + j, KR:BR, :] for j in range(count)], axis=1)
        for t in range(4):
            rows = pl.ds(t * 256, 256)
            kernel_vals = jnp.exp(dot(q[rows, :], keys)).astype(BF16)
            acc[rows, :] += dot(kernel_vals, weights, 1, 1)

    lax.fori_loop(0, 8, chunk, 0)
    with jax.named_scope("phase_far3"):
        phase_far3()
    add_keys(70, 4)

    prod_t = jnp.transpose(acc[...])
    prod_ref[...] = prod_t
    gram = dot(prod_t, acc[...], precision=lax.Precision.HIGHEST)
    g_loc[...] = jnp.concatenate([gram[0:32], gram[32:64]], axis=1)
    def gram_sib():
        return remote(g_loc.at[pl.ds(other * 16, 16)], g_sib, sib_s.at[3], sib_r.at[3], sib)

    def gram_z(d):
        return remote(g_z.at[z], g_z.at[z], rs_s.at[3], rs_r.at[3], dev(dz=d))

    def gram_plane(k):
        dx, dyl, dyh = PLANE[k]
        return remote(g_p.at[here], g_p.at[here], rs_s.at[4], rs_r.at[4], dev(dx=dx, dyl=dyl, dyh=dyh))

    def gram_back():
        mine = g_half.at[pl.ds(core * 16, 16)]
        return remote(mine, mine, sib_s.at[4], sib_r.at[4], sib)

    start(gram_sib)
    gram_sib().wait_recv()
    g_z[z] = g_loc[pl.ds(core * 16, 16)] + g_sib[...]
    for d in FARTHEST:
        start(gram_z, d)
    for c in (sib_w, sib_p, sib_x, pair_w(), pair_p()):
        c.wait_send()
    left(buf.at[pl.ds(0, 58)], slot_s.at[0])
    left(rsw.at[pl.ds(1, 7)], rs_s.at[0])
    left(rsp.at[pl.ds(1, 7)], rs_s.at[1])
    left(ag.at[pl.ds(0, 7)], rs_s.at[2])
    arrived(g_z.at[pl.ds(0, 7)], rs_r.at[3])
    total = g_z[0]
    for k in range(1, 8):
        total = total + g_z[k]
    here = (yl * 2 + yh) * 4 + x
    g_p[here] = total
    for k in range(15):
        start(gram_plane, k)
    arrived(g_p.at[pl.ds(0, 15)], rs_r.at[4])
    total = g_p[0]
    for k in range(1, 16):
        total = total + g_p[k]
    g_half[pl.ds(core * 16, 16)] = total
    start(gram_back)
    theirs = g_half.at[pl.ds(other * 16, 16)]
    remote(theirs, theirs, sib_s.at[4], sib_r.at[4], sib).wait_recv()
    gram_ref[...] = g_half[...]
    gram_sib().wait_send()
    gram_back().wait_send()
    left(g_z.at[pl.ds(0, 7)], rs_s.at[3])
    left(g_p.at[pl.ds(0, 15)], rs_s.at[4])


def split(v):
    high = v.astype(BF16)
    return high, (v - high.astype(F32)).astype(BF16)


def wide(v):
    return jnp.broadcast_to(v, (8, 128))


def tail_kernel(prod_ref, gram_ref, out_hbm, basis_ref, sem):
    copy = pltpu.make_async_copy(prod_ref, out_hbm, sem)
    copy.start()
    packed = gram_ref[...]
    gram = jnp.concatenate([packed[:, 0:R], packed[:, R : 2 * R]], axis=0)
    row = lax.broadcasted_iota(jnp.int32, (R, R), 0)
    lane = lax.broadcasted_iota(jnp.int32, (R, R), 1)
    full = jnp.concatenate([gram, (row == lane).astype(F32)], axis=1)
    rows = [full[8 * i : 8 * i + 8, :] for i in range(8)]
    sub = lax.broadcasted_iota(jnp.int32, (8, 128), 0)
    for b in range(8):
        col = {(j, i): wide(rows[i][:, 8 * b + j : 8 * b + j + 1]) for j in range(8) for i in range(b, 8)}
        diag = jnp.zeros((8, 128), F32)
        for j in range(8):
            d = wide(col[j, b][j : j + 1, :])
            inv = 1.0 / d
            diag = jnp.where(sub == j, d, diag)
            pivot = wide(rows[b][j : j + 1, :])
            heads = {n: wide(col[n, b][j : j + 1, :]) for n in range(j + 1, 8)}
            for i in range(b, 8):
                m = col[j, i] * inv
                if i == b:
                    m = jnp.where(sub > j, m, 0.0)
                rows[i] = rows[i] - m * pivot
                for n in range(j + 1, 8):
                    col[n, i] = col[n, i] - m * heads[n]
        rows[b] = rows[b] * (lax.rsqrt(diag) * 512.0)
    inverse = jnp.concatenate(rows, axis=0)[:, R : 2 * R]
    lh, ll = split(inverse)
    xh, xl = split(prod_ref[...])
    basis_ref[...] = dot(
        jnp.concatenate([lh, lh, ll], axis=1), jnp.concatenate([xh, xl, xh], axis=0)
    )
    copy.wait()


def per_device(points, vectors, leaf_interp, leaf_skeleton, group_transfer, group_skeleton):
    hbm = pl.BlockSpec(memory_space=pltpu.HBM)
    vmem = pl.BlockSpec(memory_space=pltpu.VMEM)
    dma = pltpu.SemaphoreType.DMA
    prod_t, gram = pl.pallas_call(
        main_kernel,
        out_shape=(jax.ShapeDtypeStruct((R, N), F32), jax.ShapeDtypeStruct((32, 128), F32)),
        in_specs=[hbm] * 6,
        out_specs=(vmem, vmem),
        scratch_shapes=[
            pltpu.VMEM((N, D), BF16),
            pltpu.VMEM((R, N), BF16),
            pltpu.VMEM((N, D), BF16),
            pltpu.VMEM((1, 128), jnp.int32),
            pltpu.VMEM((128, 512), BF16),
            pltpu.VMEM((1, 512), jnp.int32),
            pltpu.VMEM((SLOTS, BR, D), BF16),
            pltpu.VMEM((BR, D), BF16),
            pltpu.VMEM((2, BR, D), BF16),
            pltpu.VMEM((N, KR), BF16),
            pltpu.VMEM((N, R), F32),
            pltpu.VMEM((2, 8, 16, 128), F32),
            pltpu.VMEM((8, 16, 128), F32),
            pltpu.VMEM((2, 8, 32, 128), BF16),
            pltpu.VMEM((8, 32, 128), BF16),
            pltpu.VMEM((8, 16, 128), F32),
            pltpu.VMEM((8, 32, 128), BF16),
            pltpu.VMEM((16, 128), F32),
            pltpu.VMEM((32, 128), BF16),
            pltpu.VMEM((8, 48, 128), BF16),
            pltpu.VMEM((32, 128), F32),
            pltpu.VMEM((16, 128), F32),
            pltpu.VMEM((8, 16, 128), F32),
            pltpu.VMEM((16, 16, 128), F32),
            pltpu.VMEM((32, 128), F32),
            dma((6,)),
            dma((7,)),
            dma((7,)),
            dma((1,)),
            dma((15,)),
            dma((4,)),
            dma((14,)),
            dma((4,)),
            dma((5,)),
            dma((5,)),
        ],
        compiler_params=pltpu.CompilerParams(
            collective_id=0, has_side_effects=True, vmem_limit_bytes=40 * 2**20
        ),
        name="hss_main",
    )(
        *(
            pltpu.with_memory_space_constraint(a, pltpu.HBM)
            for a in (
                points,
                vectors.T,
                leaf_interp,
                leaf_skeleton.reshape(1, 128),
                group_transfer,
                group_skeleton.reshape(1, 512),
            )
        )
    )
    out_t, basis_t = pl.pallas_call(
        tail_kernel,
        out_shape=(jax.ShapeDtypeStruct((R, N), F32), jax.ShapeDtypeStruct((R, N), F32)),
        in_specs=[vmem, vmem],
        out_specs=(hbm, vmem),
        scratch_shapes=[pltpu.SemaphoreType.DMA],
        compiler_params=pltpu.CompilerParams(vmem_limit_bytes=16 * 2**20),
        name="hss_tail",
    )(prod_t, gram)
    return out_t.T, basis_t.T


def solution(mesh):
    spec = P(("group", "leaf"), None)
    return jax.shard_map(
        per_device,
        mesh=mesh,
        in_specs=(spec, spec, spec, P(("group", "leaf")), spec, P("group")),
        out_specs=(spec, spec),
        check_vma=False,
    )
```
